128 devices in a mesh: seq: 32 (over y, x, z_lo), col: 4 (over z_hi, core).
Axes of the slice: x: 4, y: 4, z: 4 (z_hi: 2, z_lo: 2; z = z_hi * 2 + z_lo), core: 2. Of those that a mesh axis runs over, the one named last changes fastest.
Arguments:
- q_row: bfloat16 [256, 512, 768], P('seq', 'col'), may hold values from -15 to 15
- k_row: bfloat16 [256, 512, 768], P('seq', 'col'), may hold values from -6 to 6
- v_row: bfloat16 [256, 512, 768], P('seq', 'col'), may hold values from -6 to 6
- q_col: bfloat16 [256, 512, 768], P('seq', 'col'), may hold values from -8 to 8
- k_col: bfloat16 [256, 512, 768], P('seq', 'col'), may hold values from -4 to 4
- out_grad: bfloat16 [256, 512, 768], P('seq', 'col'), may hold values from -6 to 6
Outputs:
- q_row_grad: bfloat16 [256, 512, 768], P('seq', 'col')
- k_row_grad: bfloat16 [256, 512, 768], P('seq', 'col')
- v_row_grad: bfloat16 [256, 512, 768], P('seq', 'col')
- q_col_grad: bfloat16 [256, 512, 768], P('seq', 'col')
- k_col_grad: bfloat16 [256, 512, 768], P('seq', 'col')
The draws below stay inside these ranges and needn't reach their ends.
All inputs are finite; a program needn't handle non-finite values.
Results may differ from the reference program's by a relative error of at most 0.035.
Values may be sent and summed in bfloat16 or wider, within the bound.
A program may use at most 192 MiB of HBM per device.

```python
import math
import jax
import jax.numpy as jnp
from jax import lax

H = 12
DH = 64
D = 768
COL_DEV = 128
ROWS = 256
COLS = 512
N_COL = 4


def row_base(key):
    return jax.random.truncated_normal(key, -6.0, 6.0, (ROWS, COLS, D), jnp.float32)


def col_base(key):
    return jax.random.truncated_normal(jax.random.fold_in(key, 101), -4.0, 4.0, (ROWS, COLS, D), jnp.float32)


def draw_k_row(key, part):
    base = row_base(key)
    return base.astype(jnp.bfloat16)


def draw_q_row(key, part):
    key = jax.random.fold_in(key, 5)
    return jax.random.truncated_normal(key, -6.0, 6.0, (ROWS, COLS, D), jnp.float32).astype(jnp.bfloat16)


def draw_k_col(key, part):
    base = col_base(key)
    return base.astype(jnp.bfloat16)


def draw_q_col(key, part):
    key = jax.random.fold_in(key, 9)
    return jax.random.truncated_normal(key, -4.0, 4.0, (ROWS, COLS, D), jnp.float32).astype(jnp.bfloat16)


def block_levels(key, shape, cuts, smallest, high):
    loudness = 1.0
    for dim, parts in cuts:
        draws = jax.random.uniform(jax.random.fold_in(jax.random.fold_in(key, 6), dim), (parts,), jnp.float32, smallest / len(cuts), high / len(cuts))
        loudness = loudness * jnp.repeat(jnp.exp(draws), shape[dim] // parts).reshape((-1,) + (1,) * (len(shape) - 1 - dim))
    return loudness


def scatter_about(own_key, extent, scale, reach, cuts=(), kind=jnp.bfloat16):
    drawn = scale * jax.random.normal(own_key, extent, jnp.float32)
    if cuts:
        drawn = drawn * block_levels(own_key, extent, cuts, -0.22, 0.18)
    return jnp.clip(drawn, -reach, reach).astype(kind)


def setup_inputs(seed: int = 0) -> dict:
    seeds = jax.random.split(jax.random.key(seed), 7)
    q_row = draw_q_row(jax.random.fold_in(seeds[6], 71), 0)
    k_row = draw_k_row(jax.random.fold_in(seeds[6], 71), 0)
    v_row = scatter_about(seeds[2], (ROWS, COLS, D), 1.0, 6.0, ((0, 32), (1, 4)))
    q_col = draw_q_col(jax.random.fold_in(seeds[6], 71), 0)
    k_col = draw_k_col(jax.random.fold_in(seeds[6], 71), 0)
    out_grad = scatter_about(seeds[5], (ROWS, COLS, D), 1.0, 6.0, ((0, 32), (1, 4)))
    return {"q_row": q_row, "k_row": k_row, "v_row": v_row, "q_col": q_col, "k_col": k_col, "out_grad": out_grad}


def upcast(tensor):
    return tensor.astype(jnp.float32)

def rounded(tensor):
    return upcast(lax.optimization_barrier(tensor.astype(jnp.bfloat16)))

def softmax_rows(scores):
    largest = lax.optimization_barrier(jnp.max(scores, axis=-1, keepdims=True))
    weights = jnp.exp(scores - largest)
    return weights / lax.optimization_barrier(jnp.sum(weights, axis=-1, keepdims=True))

def slope_rows(probabilities, gradients):
    return probabilities * (gradients - lax.optimization_barrier(jnp.sum(probabilities * gradients, axis=-1, keepdims=True)))

def head_grads(inputs):
    queries, keys_row, values_row, col_queries, col_keys, cotangent = [upcast(item) for item in inputs]
    row_total = queries.shape[0]
    col_total = queries.shape[1]
    row_scale = 1.0 / math.sqrt(DH * row_total)
    col_scale = 1.0 / math.sqrt(DH)
    tied = softmax_rows(jnp.einsum('rie,rje->ij', queries, keys_row) * row_scale)
    tied_half = rounded(tied)
    row_output = rounded(jnp.einsum('ij,rje->rie', tied_half, values_row))
    col_probs = softmax_rows(jnp.einsum('rce,sce->crs', col_queries, col_keys) * col_scale)
    col_half = rounded(col_probs)
    col_grads = jnp.einsum('rce,sce->crs', cotangent, row_output)
    col_slopes = rounded(slope_rows(col_probs, col_grads))
    mixed_grad = rounded(jnp.einsum('crs,rce->sce', col_half, cotangent))
    q_col_grad = (jnp.einsum('crs,sce->rce', col_slopes, col_keys) * col_scale).astype(jnp.bfloat16)
    k_col_grad = (jnp.einsum('crs,rce->sce', col_slopes, col_queries) * col_scale).astype(jnp.bfloat16)
    tied_grads = jnp.einsum('rie,rje->ij', mixed_grad, values_row)
    tied_slopes = rounded(slope_rows(tied, tied_grads))
    q_row_grad = (jnp.einsum('ij,rje->rie', tied_slopes, keys_row) * row_scale).astype(jnp.bfloat16)
    slope_blocks = tied_slopes.reshape(N_COL, COL_DEV, col_total)
    prob_blocks = tied_half.reshape(N_COL, COL_DEV, col_total)
    query_blocks = queries.reshape(row_total, N_COL, COL_DEV, DH)
    grad_blocks = mixed_grad.reshape(row_total, N_COL, COL_DEV, DH)
    key_parts = rounded(jnp.einsum('bij,rbie->brje', slope_blocks, query_blocks) * row_scale)
    value_parts = rounded(jnp.einsum('bij,rbie->brje', prob_blocks, grad_blocks))
    k_row_grad = lax.optimization_barrier(jnp.sum(key_parts, axis=0)).astype(jnp.bfloat16)
    v_row_grad = lax.optimization_barrier(jnp.sum(value_parts, axis=0)).astype(jnp.bfloat16)
    return (q_row_grad, k_row_grad, v_row_grad, q_col_grad, k_col_grad)

def heads_first(tensor):
    return tensor.reshape(ROWS, COLS, H, DH).transpose(2, 0, 1, 3)

def heads_last(tensor):
    return tensor.transpose(1, 2, 0, 3).reshape(ROWS, COLS, H * DH)

def reference(q_row, k_row, v_row, q_col, k_col, out_grad):
    stacked = lax.map(head_grads, (heads_first(q_row), heads_first(k_row), heads_first(v_row), heads_first(q_col), heads_first(k_col), heads_first(out_grad)))
    return (heads_last(stacked[0]), heads_last(stacked[1]), heads_last(stacked[2]), heads_last(stacked[3]), heads_last(stacked[4]))
```

```python
import math

import jax
import jax.numpy as jnp
from jax import lax
from jax.experimental import pallas as pl
from jax.experimental.pallas import tpu as pltpu
from jax.sharding import PartitionSpec as P

MESH = pl.DeviceIdType.MESH
F32 = jnp.float32
BF16 = jnp.bfloat16
NT = (((1,), (1,)), ((), ()))
NN = (((1,), (0,)), ((), ()))
TN = (((0,), (0,)), ((), ()))
ROW_SCALE = 1.0 / math.sqrt(16384.0)
COL_SCALE = 1.0 / math.sqrt(64.0)


def dot(a, b, dims):
    return lax.dot_general(a, b, dims, preferred_element_type=F32)


def swap_halves(t):
    return jnp.concatenate([t[..., 64:128], t[..., 0:64]], axis=-1)


def low_lanes(shape):
    return lax.broadcasted_iota(jnp.int32, shape, len(shape) - 1) % 128 < 64


def pack(src, dst):
    lo = low_lanes((128, 128))

    def step(r2, _):
        for half in range(2):
            base = half * 384
            first_a, first_b = src[r2, :, base : base + 128], src[r2 + 4, :, base : base + 128]
            mid_a, mid_b = src[r2, :, base + 128 : base + 256], src[r2 + 4, :, base + 128 : base + 256]
            last_a, last_b = src[r2, :, base + 256 : base + 384], src[r2 + 4, :, base + 256 : base + 384]
            turned = swap_halves(mid_b)
            even, odd = 2 * half, 2 * half + 1
            dst[even, r2, :, 0:128] = first_a
            dst[even, r2, :, 128:256] = jnp.where(lo, mid_a, turned)
            dst[even, r2, :, 256:384] = first_b
            dst[odd, r2, :, 0:128] = last_a
            dst[odd, r2, :, 128:256] = jnp.where(lo, turned, mid_a)
            dst[odd, r2, :, 256:384] = last_b
        return 0

    lax.fori_loop(0, 4, step, 0)


def unpack_kernel(*refs):
    lo = low_lanes((128, 128))
    for src, dst in zip(refs[:5], refs[5:]):
        for half in range(2):
            base = half * 384
            even, odd = 2 * half, 2 * half + 1
            mid_even, mid_odd = src[even, 0, :, 128:256], src[odd, 0, :, 128:256]
            dst[0, 0, :, base : base + 128] = src[even, 0, :, 0:128]
            dst[1, 0, :, base : base + 128] = src[even, 0, :, 256:384]
            dst[0, 0, :, base + 128 : base + 256] = jnp.where(lo, mid_even, mid_odd)
            dst[1, 0, :, base + 128 : base + 256] = swap_halves(jnp.where(lo, mid_odd, mid_even))
            dst[0, 0, :, base + 256 : base + 384] = src[odd, 0, :, 0:128]
            dst[1, 0, :, base + 256 : base + 384] = src[odd, 0, :, 256:384]


def unpack(packed):
    outs = pl.pallas_call(
        unpack_kernel,
        name="unpack",
        grid=(4,),
        out_shape=[jax.ShapeDtypeStruct((2, 4, 128, 768), BF16)] * 5,
        in_specs=[pl.BlockSpec((4, 1, 128, 384), lambda i: (0, i, 0, 0))] * 5,
        out_specs=[pl.BlockSpec((2, 1, 128, 768), lambda i: (0, i, 0, 0))] * 5,
    )(*packed)
    return tuple(o.reshape(8, 128, 768) for o in outs)


def row_products(a, b, out):
    low = low_lanes((512, 512))
    zero = jnp.zeros((512, 512), BF16)
    for pair in range(2):
        u, v = 2 * pair, 2 * pair + 1
        left = jnp.concatenate([a[u, :, 0:128], a[u, :, 256:384], a[v, :, 0:128], a[v, :, 256:384]], axis=1)
        right = jnp.concatenate([b[u, :, 0:128], b[u, :, 256:384], b[v, :, 0:128], b[v, :, 256:384]], axis=1)
        first = dot(jnp.where(low, left, zero), right, NT)
        second = dot(jnp.where(low, zero, left), right, NT)
        left = jnp.concatenate([a[u, :, 128:256], a[v, :, 128:256]], axis=1)
        right = jnp.concatenate([b[u, :, 128:256], b[v, :, 128:256]], axis=1)
        third = dot(left, right, NT)
        if pair == 0:
            out[0], out[1], out[2] = first, second, third
        else:
            out[0] += first
            out[1] += second
            out[2] += third


def row_apply(m, b, store, dims, scale=None):
    low = low_lanes((512, 256))

    def step(pair, _):
        for r2 in (2 * pair, 2 * pair + 1):
            right = jnp.concatenate([b[r2, :, 0:128], b[r2, :, 256:384]], axis=1)
            both = jnp.where(low, dot(m[0], right, dims), dot(m[1], right, dims))
            if scale is not None:
                both = both * scale
            both = both.astype(BF16)
            store(r2, 0, both[:, 0:128])
            store(r2, 2, both[:, 128:256])
        right = jnp.concatenate([b[2 * pair, :, 128:256], b[2 * pair + 1, :, 128:256]], axis=1)
        third = dot(m[2], right, dims)
        if scale is not None:
            third = third * scale
        third = third.astype(BF16)
        store(2 * pair, 1, third[:, 0:128])
        store(2 * pair + 1, 1, third[:, 128:256])
        return 0

    lax.fori_loop(0, 2, step, 0)


def by_column(src, wide, dst):
    def widen(i, _):
        rows = pl.multiple_of(i * 16, 16)
        block = src[pl.ds(rows, 16)].reshape(256, 384).astype(F32)
        for t in range(3):
            wide[t, pl.ds(pl.multiple_of(i * 256, 256), 256), :] = block[:, 128 * t : 128 * t + 128]
        return 0

    lax.fori_loop(0, 8, widen, 0)

    def gather(c, _):
        for t in range(3):
            dst[c, :, 128 * t : 128 * t + 128] = wide[t, pl.ds(c, 128, stride=16), :].astype(BF16)
        return 0

    lax.fori_loop(0, 16, gather, 0)


def by_row(wide, dst):
    def narrow(i, _):
        rows = pl.multiple_of(i * 16, 16)
        for t in range(3):
            block = wide[t, pl.ds(pl.multiple_of(i * 256, 256), 256), :]
            dst[pl.ds(rows, 16), :, 128 * t : 128 * t + 128] = block.astype(BF16).reshape(16, 16, 128)
        return 0

    lax.fori_loop(0, 8, narrow, 0)


def stacks(ref, c):
    outer = jnp.concatenate([ref[c, :, 0:128], ref[c, :, 256:384]], axis=0)
    mid = ref[c, :, 128:256]
    return outer, jnp.concatenate([mid, swap_halves(mid)], axis=0)


def keep(x, low):
    lo = low_lanes(x.shape)
    zero = jnp.zeros_like(x)
    return jnp.where(lo, x, zero) if low else jnp.where(lo, zero, x)


def col_probs(keys, queries):
    scores = dot(keys, queries, NT) * COL_SCALE
    weights = jnp.exp(scores - jnp.max(scores, axis=0, keepdims=True))
    return weights / jnp.sum(weights, axis=0, keepdims=True)


def put_column(wide, c, p_part, q_part, w_part):
    lo = low_lanes((256, 128))
    outer = jnp.where(lo, p_part, q_part)
    rows = pl.ds(c, 128, stride=16)
    wide[0, rows, :] = outer[0:128]
    wide[2, rows, :] = outer[128:256]
    wide[1, rows, :] = jnp.where(lo[0:128], w_part[0:128], swap_halves(w_part[128:256]))


def main_kernel(
    q_row, k_row, v_row, q_col, k_col, out_grad,
    o_qr, o_kr, o_vr, o_qc, o_kc,
    stage, sends, rq, rk, rv, cq, ck, co, cro, rmix,
    part, core_l, core_g, sum_l, half_g, sum_g, tied_f, tied, slopes,
    wide0, wide1, col_q, col_k, col_o, col_r,
    load_sem, in_send, in_recv, plane_send, plane_recv, core_send, core_recv, out_send, out_recv,
):
    s, g = lax.axis_index("seq"), lax.axis_index("col")
    x, y, zl = (s // 2) % 4, s // 8, s % 2
    zh, core = g // 2, g % 2
    z = 2 * zh + zl
    chip = y * 4 + x
    slab = core * 16 + chip

    def dev(x_, y_, z_, core_):
        return (y_ * 8 + x_ * 2 + z_ % 2, (z_ // 2) * 2 + core_)

    def is_me(d):
        return jnp.logical_and(d[0] == s, d[1] == g)

    def push(src, dst, send_sem, recv_sem, dest, maybe_me=True):
        def remote():
            pltpu.make_async_remote_copy(
                src_ref=src, dst_ref=dst, send_sem=send_sem, recv_sem=recv_sem, device_id=dest, device_id_type=MESH
            ).start()

        if not maybe_me:
            remote()
            return
        me = is_me(dest)
        pl.when(jnp.logical_not(me))(remote)

        @pl.when(me)
        def _():
            pltpu.make_async_copy(src, dst, recv_sem).start()

    def wait_for(ref, sem):
        pltpu.make_async_copy(ref, ref, sem).wait()

    def loop(n, body):
        def step(i, _):
            body(i)
            return 0

        lax.fori_loop(0, n, step, 0)

    def row_dest(i):
        return dev(x, y, (z + i) % 4, zl)

    def row_home(i):
        return dev(x, y, 2 * (i // 2) + core, i % 2), i

    def col_dest(i):
        m = (i // 4 + s) % 8
        z_ = (z + i) % 4
        return dev(m % 4, 2 * core + m // 4, z_, zh), m, z_

    def col_home(i):
        j = (s + i) % 32
        return (j, core * 2 + y // 2), j

    def plane_dest(i):
        x_, y_, core_ = (x + i) % 4, (y + (i // 4)) % 4, (core + i // 16) % 2
        return dev(x_, y_, z, core_), x_, y_, core_

    barrier = pltpu.get_barrier_semaphore()

    def greet(dest):
        @pl.when(jnp.logical_not(is_me(dest)))
        def _():
            pl.semaphore_signal(barrier, inc=1, device_id=dest, device_id_type=MESH)

    arrays = (q_row, k_row, q_col, k_col, out_grad, v_row)

    def load(n):
        return pltpu.make_async_copy(arrays[n], stage.at[n % 2], load_sem.at[n % 2])

    load(0).start()
    load(1).start()
    loop(4, lambda i: greet(row_dest(i)))
    loop(4, lambda i: greet(row_home(i)[0]))
    loop(32, lambda i: greet(col_dest(i)[0]))
    loop(32, lambda i: greet(col_home(i)[0]))
    loop(32, lambda i: greet(plane_dest(i)[0]))
    own = jnp.where(core == zl, 2, 0) + jnp.where(jnp.logical_and(core == zh, y // 2 == core), 2, 0)
    pl.semaphore_wait(barrier, 103 - own)

    def send_rows(n, dst):
        def body(i):
            z_ = (z + i) % 4
            push(sends.at[n, z_], dst.at[:, pl.ds(pl.multiple_of(g * 128, 128), 128), :],
                 in_send.at[n], in_recv.at[n], row_dest(i))

        loop(4, body)

    def send_cols(n, dst):
        def body(i):
            dest, m, z_ = col_dest(i)
            push(sends.at[n, z_, :, pl.ds(pl.multiple_of(m * 16, 16), 16), :],
                 dst.at[pl.ds(4 * s, 4)], in_send.at[n], in_recv.at[n], dest)

        loop(32, body)

    for n, dst in enumerate((rq, rk, cq, ck, co, rv)):
        load(n).wait()
        pack(stage.at[n % 2], sends.at[n])
        if n + 2 < 6:
            load(n + 2).start()
        if n in (0, 1, 5):
            send_rows(n, dst)
        else:
            send_cols(n, dst)

    own_rows = pl.ds(pl.multiple_of(core * 256, 256), 256)
    other_rows = pl.ds(pl.multiple_of((1 - core) * 256, 256), 256)
    own_slab = pl.ds(pl.multiple_of(slab * 16, 16), 16)
    other_core = dev(x, y, z, 1 - core)

    def wait_plane(n, ref, other):
        wait_for(ref, plane_send.at[n])
        wait_for(other, plane_recv.at[n])

    wait_for(rq, in_recv.at[0])
    wait_for(rk, in_recv.at[1])
    row_products(rq, rk, part)
    push(part.at[:, other_rows, :], core_l, core_send.at[0], core_recv.at[0], other_core, False)
    wait_for(core_l, core_recv.at[0])
    part[:, own_rows, :] += core_l[...]

    def send_sum(i, src, dst, n):
        dest, x_, y_, _ = plane_dest(i)
        rows = pl.ds(pl.multiple_of((y_ * 4 + x_) * 16, 16), 16)
        push(src(rows, y_ * 4 + x_), dst.at[chip], plane_send.at[n], plane_recv.at[n], dest)

    def part_rows(rows, n):
        return part.at[:, pl.ds(pl.multiple_of(core * 256 + n * 16, 16), 16), :]

    loop(16, lambda i: send_sum(i, part_rows, sum_l, 0))
    wait_for(sum_l, plane_recv.at[0])
    logits = sum_l[0]
    for n in range(1, 16):
        logits += sum_l[n]
    logits = logits * ROW_SCALE
    weights = jnp.exp(logits - jnp.max(logits, axis=-1, keepdims=True))
    probs = weights / jnp.sum(weights, axis=-1, keepdims=True)
    tied_f[...] = probs

    def share(value, dst, n, core_n):
        dst[:, own_slab, :] = value.astype(BF16)
        loop(15, lambda i: push(dst.at[:, own_slab, :], dst.at[:, own_slab, :], plane_send.at[n], plane_recv.at[n],
                                plane_dest(i + 1)[0], False))
        wait_for(dst.at[:, 0:240, :], plane_recv.at[n])
        push(dst.at[:, own_rows, :], dst.at[:, own_rows, :], core_send.at[core_n], core_recv.at[core_n], other_core, False)
        wait_for(dst.at[:, 0:256, :], core_recv.at[core_n])

    share(probs, tied, 1, 1)

    wait_for(rv, in_recv.at[5])

    def wait_sent_in(n, chunk, count, mine):
        @pl.when(mine)
        def _():
            wait_for(chunk(count - 1), in_send.at[n])

        @pl.when(jnp.logical_not(mine))
        def _():
            wait_for(chunk(count), in_send.at[n])

    row_mine = core == zl
    col_mine = jnp.logical_and(core == zh, y // 2 == core)
    wait_sent_in(5, lambda k: sends.at[5, 0:k], 4, row_mine)

    ro = sends.at[5]

    def put_ro(r2, tile, value):
        for b in range(4):
            ro[r2, b, :, tile * 128 : tile * 128 + 128] = value[128 * b : 128 * b + 128]

    row_apply(tied, rv, put_ro, NN)

    def send_ro(i):
        dest, x_, y_, core_ = plane_dest(i)
        t = core_ * 16 + y_ * 4 + x_
        push(ro.at[:, t // 8, pl.ds(pl.multiple_of((t % 8) * 16, 16), 16), :], cro.at[pl.ds(4 * (chip * 2 + core), 4)],
             plane_send.at[2], plane_recv.at[2], dest)

    loop(32, send_ro)

    wait_for(cq, in_recv.at[2])
    wait_for(ck, in_recv.at[3])
    wait_for(co, in_recv.at[4])
    by_column(cq, wide0, col_q)
    by_column(ck, wide0, col_k)
    by_column(co, wide0, col_o)

    def first_pass(c):
        q, qw = stacks(col_q, c)
        k, kw = stacks(col_k, c)
        o, ow = stacks(col_o, c)
        parts = []
        for keys, queries, cot in ((k, keep(q, True), o), (k, keep(q, False), o), (kw, keep(qw, True), ow)):
            parts.append(dot(col_probs(keys, queries).astype(BF16), cot, NN))
        put_column(wide1, c, *parts)

    loop(16, first_pass)
    by_row(wide1, cq)

    def send_col(src, dst, send_sem, recv_sem):
        def body(i):
            dest, x_, y_, core_ = plane_dest(i)
            push(src.at[pl.ds(4 * ((y_ * 4 + x_) * 2 + core_), 4)], dst.at[:, own_slab, :], send_sem, recv_sem, dest)

        loop(32, body)

    send_col(cq, rmix, plane_send.at[3], plane_recv.at[3])

    wait_for(cro, plane_recv.at[2])
    by_column(cro, wide0, col_r)

    def second_pass(c):
        q, qw = stacks(col_q, c)
        k, kw = stacks(col_k, c)
        o, ow = stacks(col_o, c)
        r, rw = stacks(col_r, c)
        q_parts, k_parts = [], []
        for keys, queries, cot, vals, low in ((k, q, o, r, True), (k, q, o, r, False), (kw, qw, ow, rw, True)):
            probs = col_probs(keys, keep(queries, low))
            grads = dot(vals, keep(cot, low), NT)
            slope = probs * (grads - jnp.sum(probs * grads, axis=0, keepdims=True))
            slope = slope.astype(BF16)
            k_parts.append(dot(slope, queries, NN) * COL_SCALE)
            q_parts.append(dot(slope, keys, TN) * COL_SCALE)
        put_column(wide0, c, *q_parts)
        put_column(wide1, c, *k_parts)

    loop(16, second_pass)
    by_row(wide0, ck)
    by_row(wide1, co)

    def send_home(src, dst, n):
        def body(i):
            dest, j = col_home(i)
            push(src.at[pl.ds(4 * j, 4)], dst.at[z, :, pl.ds(pl.multiple_of((slab % 8) * 16, 16), 16), :],
                 out_send.at[n], out_recv.at[n], dest)

        loop(32, body)

    send_home(ck, o_qc, 3)
    send_home(co, o_kc, 4)

    wait_for(rmix, plane_recv.at[3])
    wait_for(part.at[:, 0:256, :], core_send.at[0])
    wait_for(sum_l.at[0:15], plane_send.at[0])
    row_products(rmix, rv, part)
    push(part.at[:, other_rows, :], core_g, core_send.at[2], core_recv.at[2], other_core, False)
    wait_for(core_g, core_recv.at[2])
    half_g[...] = (part[:, own_rows, :] + core_g[...]).astype(BF16)

    def half_rows(rows, n):
        return half_g.at[:, rows, :]

    loop(16, lambda i: send_sum(i, half_rows, sum_g, 4))

    def in_place(ref):
        def store(r2, tile, value):
            ref[r2, :, tile * 128 : tile * 128 + 128] = value

        return store

    def send_rows_home(src, dst, n):
        def body(i):
            dest, b = row_home(i)
            push(src.at[:, pl.ds(pl.multiple_of(b * 128, 128), 128), :], dst.at[z], out_send.at[n], out_recv.at[n], dest)

        loop(4, body)

    row_apply(tied, rmix, in_place(rmix), TN)
    send_rows_home(rmix, o_vr, 2)

    wait_for(sum_g, plane_recv.at[4])
    grads = sum_g[0].astype(F32)
    for n in range(1, 16):
        grads += sum_g[n].astype(F32)
    probs = tied_f[...]
    slope = probs * (grads - jnp.sum(probs * grads, axis=-1, keepdims=True))
    share(slope, slopes, 5, 3)

    row_apply(slopes, rk, in_place(rk), NN, ROW_SCALE)
    send_rows_home(rk, o_qr, 0)
    row_apply(slopes, rq, in_place(rq), TN, ROW_SCALE)
    send_rows_home(rq, o_kr, 1)

    for n in (0, 1):
        wait_sent_in(n, lambda k, n=n: sends.at[n, 0:k], 4, row_mine)
    for n in (2, 3, 4):
        wait_sent_in(n, lambda k: cq.at[0 : 4 * k], 32, col_mine)
    wait_for(tied.at[:, 0:240, :], plane_send.at[1])
    wait_for(cro.at[0:124], plane_send.at[2])
    wait_for(cro.at[0:124], plane_send.at[3])
    wait_for(sum_g.at[0:15], plane_send.at[4])
    wait_for(tied.at[:, 0:240, :], plane_send.at[5])
    wait_for(tied.at[:, 0:256, :], core_send.at[1])
    wait_for(core_g, core_send.at[2])
    wait_for(tied.at[:, 0:256, :], core_send.at[3])

    def wait_out(n, chunk, count, mine):
        @pl.when(mine)
        def _():
            wait_for(chunk(count - 1), out_send.at[n])

        @pl.when(jnp.logical_not(mine))
        def _():
            wait_for(chunk(count), out_send.at[n])

    for n, ref in enumerate((o_qr, o_kr, o_vr, o_qc, o_kc)):
        if n < 3:
            wait_out(n, lambda k: sends.at[n, 0:k], 4, row_mine)
        else:
            wait_out(n, lambda k: cq.at[0 : 4 * k], 32, col_mine)
        wait_for(ref, out_recv.at[n])


def on_device(q_row, k_row, v_row, q_col, k_col, out_grad):
    vm = pltpu.VMEM
    dma = pltpu.SemaphoreType.DMA
    rows, cols = (4, 512, 384), (128, 16, 384)
    packed = pl.pallas_call(
        main_kernel,
        name="layer",
        out_shape=[jax.ShapeDtypeStruct((4, 4, 128, 384), BF16)] * 5,
        in_specs=[pl.BlockSpec(memory_space=pl.ANY)] * 6,
        out_specs=[pl.BlockSpec(memory_space=pl.ANY)] * 5,
        scratch_shapes=[
            vm((2, 8, 128, 768), BF16),
            vm((6, 4, 4, 128, 384), BF16),
            vm(rows, BF16), vm(rows, BF16), vm(rows, BF16),
            vm(cols, BF16), vm(cols, BF16), vm(cols, BF16), vm(cols, BF16),
            vm(rows, BF16),
            vm((3, 512, 512), F32),
            vm((3, 256, 512), F32), vm((3, 256, 512), F32),
            vm((16, 3, 16, 512), F32),
            vm((3, 256, 512), BF16),
            vm((16, 3, 16, 512), BF16),
            vm((3, 16, 512), F32),
            vm((3, 512, 512), BF16), vm((3, 512, 512), BF16),
            vm((3, 2048, 128), F32), vm((3, 2048, 128), F32),
            vm((16, 128, 384), BF16), vm((16, 128, 384), BF16), vm((16, 128, 384), BF16), vm((16, 128, 384), BF16),
            dma((2,)), dma((6,)), dma((6,)), dma((6,)), dma((6,)), dma((4,)), dma((4,)), dma((5,)), dma((5,)),
        ],
        compiler_params=pltpu.CompilerParams(collective_id=0, has_side_effects=True, vmem_limit_bytes=62 << 20),
    )(q_row, k_row, v_row, q_col, k_col, out_grad)
    return unpack(packed)


def solution(mesh):
    spec = P("seq", "col", None)
    return jax.shard_map(on_device, mesh=mesh, in_specs=(spec,) * 6, out_specs=(spec,) * 5, check_vma=False)
```

```python
import math

import jax
import jax.numpy as jnp
from jax import lax
from jax.experimental import pallas as pl
from jax.experimental.pallas import tpu as pltpu
from jax.sharding import PartitionSpec as P

MESH = pl.DeviceIdType.MESH
F32 = jnp.float32
BF16 = jnp.bfloat16
NT = (((1,), (1,)), ((), ()))
NN = (((1,), (0,)), ((), ()))
TN = (((0,), (0,)), ((), ()))
ROW_SCALE = 1.0 / math.sqrt(16384.0)
COL_SCALE = 1.0 / math.sqrt(64.0)


def dot(a, b, dims):
    return lax.dot_general(a, b, dims, preferred_element_type=F32)


def swap_halves(t):
    return jnp.concatenate([t[..., 64:128], t[..., 0:64]], axis=-1)


def low_lanes(shape):
    return lax.broadcasted_iota(jnp.int32, shape, len(shape) - 1) % 128 < 64


def pack(src, dst):
    lo = low_lanes((128, 128))

    def step(r2, _):
        for half in range(2):
            base = half * 384
            mid_a, mid_b = src[r2, :, base + 128 : base + 256], src[r2 + 4, :, base + 128 : base + 256]
            turned = swap_halves(mid_b)
            even, odd = 2 * half, 2 * half + 1
            dst[even, r2, :, 0:128] = src[r2, :, base : base + 128]
            dst[even, r2, :, 128:256] = src[r2 + 4, :, base : base + 128]
            dst[even, r2, :, 256:384] = jnp.where(lo, mid_a, turned)
            dst[odd, r2, :, 0:128] = src[r2, :, base + 256 : base + 384]
            dst[odd, r2, :, 128:256] = src[r2 + 4, :, base + 256 : base + 384]
            dst[odd, r2, :, 256:384] = jnp.where(lo, turned, mid_a)
        return 0

    lax.fori_loop(0, 4, step, 0)


def unpack_kernel(*refs):
    lo = low_lanes((128, 128))
    for src, dst in zip(refs[:5], refs[5:]):
        for half in range(2):
            base = half * 384
            even, odd = 2 * half, 2 * half + 1
            mid_even, mid_odd = src[even, 0, :, 256:384], src[odd, 0, :, 256:384]
            dst[0, 0, :, base : base + 128] = src[even, 0, :, 0:128]
            dst[1, 0, :, base : base + 128] = src[even, 0, :, 128:256]
            dst[0, 0, :, base + 128 : base + 256] = jnp.where(lo, mid_even, mid_odd)
            dst[1, 0, :, base + 128 : base + 256] = swap_halves(jnp.where(lo, mid_odd, mid_even))
            dst[0, 0, :, base + 256 : base + 384] = src[odd, 0, :, 0:128]
            dst[1, 0, :, base + 256 : base + 384] = src[odd, 0, :, 128:256]


def unpack(packed):
    outs = pl.pallas_call(
        unpack_kernel,
        name="unpack",
        grid=(4,),
        out_shape=[jax.ShapeDtypeStruct((2, 4, 128, 768), BF16)] * 5,
        in_specs=[pl.BlockSpec((4, 1, 128, 384), lambda i: (0, i, 0, 0))] * 5,
        out_specs=[pl.BlockSpec((2, 1, 128, 768), lambda i: (0, i, 0, 0))] * 5,
    )(*packed)
    return tuple(o.reshape(8, 128, 768) for o in outs)


def row_products(a, b, out):
    low = low_lanes((512, 512))
    zero = jnp.zeros((512, 512), BF16)
    for pair in range(2):
        u, v = 2 * pair, 2 * pair + 1
        left = jnp.concatenate([a[u, :, 0:256], a[v, :, 0:256]], axis=1)
        right = jnp.concatenate([b[u, :, 0:256], b[v, :, 0:256]], axis=1)
        first = dot(jnp.where(low, left, zero), right, NT)
        second = dot(jnp.where(low, zero, left), right, NT)
        left = jnp.concatenate([a[u, :, 256:384], a[v, :, 256:384]], axis=1)
        right = jnp.concatenate([b[u, :, 256:384], b[v, :, 256:384]], axis=1)
        third = dot(left, right, NT)
        if pair == 0:
            out[0], out[1], out[2] = first, second, third
        else:
            out[0] += first
            out[1] += second
            out[2] += third


def row_apply(m, b, store, dims, scale=None):
    low = low_lanes((512, 256))

    def step(pair, _):
        for r2 in (2 * pair, 2 * pair + 1):
            right = b[r2, :, 0:256]
            both = jnp.where(low, dot(m[0], right, dims), dot(m[1], right, dims))
            if scale is not None:
                both = both * scale
            both = both.astype(BF16)
            store(r2, 0, both[:, 0:128])
            store(r2, 1, both[:, 128:256])
        right = jnp.concatenate([b[2 * pair, :, 256:384], b[2 * pair + 1, :, 256:384]], axis=1)
        third = dot(m[2], right, dims)
        if scale is not None:
            third = third * scale
        third = third.astype(BF16)
        store(2 * pair, 2, third[:, 0:128])
        store(2 * pair + 1, 2, third[:, 128:256])
        return 0

    lax.fori_loop(0, 2, step, 0)


def by_column(src, wide, dst):
    def widen(i, _):
        block = src[i // 4, pl.ds((i % 4) * 4, 4)].reshape(256, 384).astype(F32)
        for t in range(3):
            wide[t, pl.ds(pl.multiple_of(i * 256, 256), 256), :] = block[:, 128 * t : 128 * t + 128]
        return 0

    lax.fori_loop(0, 8, widen, 0)

    def gather(c, _):
        for t in range(3):
            dst[c, :, 128 * t : 128 * t + 128] = wide[t, pl.ds(c, 128, stride=16), :].astype(BF16)
        return 0

    lax.fori_loop(0, 16, gather, 0)


def by_row(wide, dst, tiles):
    def narrow(i, _):
        for t in tiles:
            block = wide[t, pl.ds(pl.multiple_of(i * 256, 256), 256), :].astype(BF16)
            dst[i // 4, pl.ds((i % 4) * 4, 4), :, :, 128 * t : 128 * t + 128] = block.reshape(4, 4, 16, 128)
        return 0

    lax.fori_loop(0, 8, narrow, 0)


def outer_rows(ref, c):
    return jnp.concatenate([ref[c, :, 0:128], ref[c, :, 128:256]], axis=0)


def mid_rows(ref, c):
    mid = ref[c, :, 256:384]
    return jnp.concatenate([mid, swap_halves(mid)], axis=0)


def keep(x, low):
    lo = low_lanes(x.shape)
    zero = jnp.zeros_like(x)
    return jnp.where(lo, x, zero) if low else jnp.where(lo, zero, x)


HEADS = ((outer_rows, True), (outer_rows, False), (mid_rows, True))


def put_outer(wide, c, p_part, q_part):
    outer = jnp.where(low_lanes((256, 128)), p_part, q_part)
    rows = pl.ds(c, 128, stride=16)
    wide[0, rows, :] = outer[0:128]
    wide[1, rows, :] = outer[128:256]


def put_mid(wide, c, part):
    wide[2, pl.ds(c, 128, stride=16), :] = jnp.where(low_lanes((128, 128)), part[0:128], swap_halves(part[128:256]))


def main_kernel(
    q_row, k_row, v_row, q_col, k_col, out_grad,
    o_qr, o_kr, o_vr, o_qc, o_kc,
    stage, sends, rq, rk, rv, mq, mk, mo, cq, ck, co, cro, rmix,
    part, core_l, core_g, sum_l, half_g, sum_g, tied_f, tied, slopes,
    wide0, wide1, col_q, col_k, col_o, col_r, norms,
    load_sem, in_send, in_recv, on_send, on_recv, plane_send, plane_recv, core_send, core_recv, out_send, out_recv,
):
    s, g = lax.axis_index("seq"), lax.axis_index("col")
    x, y, zl = (s // 2) % 4, s // 8, s % 2
    zh, core = g // 2, g % 2
    z = 2 * zh + zl
    chip = y * 4 + x
    slab = core * 16 + chip

    def dev(x_, y_, z_, core_):
        return (y_ * 8 + x_ * 2 + z_ % 2, (z_ // 2) * 2 + core_)

    def is_me(d):
        return jnp.logical_and(d[0] == s, d[1] == g)

    def push(src, dst, send_sem, recv_sem, dest, maybe_me=True):
        def remote():
            pltpu.make_async_remote_copy(
                src_ref=src, dst_ref=dst, send_sem=send_sem, recv_sem=recv_sem, device_id=dest, device_id_type=MESH
            ).start()

        if not maybe_me:
            remote()
            return
        me = is_me(dest)
        pl.when(jnp.logical_not(me))(remote)

        @pl.when(me)
        def _():
            pltpu.make_async_copy(src, dst, recv_sem).start()

    def wait_for(ref, sem):
        pltpu.make_async_copy(ref, ref, sem).wait()

    def wait_sent(sem, chunks, count, mine):
        @pl.when(mine)
        def _():
            wait_for(chunks(count - 1), sem)

        @pl.when(jnp.logical_not(mine))
        def _():
            wait_for(chunks(count), sem)

    def loop(n, body):
        def step(i, _):
            body(i)
            return 0

        lax.fori_loop(0, n, step, 0)

    row_mine = core == zl
    plane_mine = y // 2 == core
    line_mine = core == zh
    home_mine = jnp.logical_and(line_mine, plane_mine)

    def row_dest(i):
        return dev(x, y, (z + i) % 4, zl)

    def row_home(i):
        return dev(x, y, 2 * (i // 2) + core, i % 2), i

    def col_dest(i):
        m = (i // 4 + s) % 8
        return dev(m % 4, 2 * core + m // 4, (z + i) % 4, zh)

    def col_home(i):
        j = (s + i) % 32
        return (j, core * 2 + y // 2), j

    def plane_dest(i):
        x_, y_, core_ = (x + i) % 4, (y + (i // 4)) % 4, (core + i // 16) % 2
        return dev(x_, y_, z, core_), x_, y_, core_

    barrier = pltpu.get_barrier_semaphore()

    def greet(dest):
        @pl.when(jnp.logical_not(is_me(dest)))
        def _():
            pl.semaphore_signal(barrier, inc=1, device_id=dest, device_id_type=MESH)

    arrays = (q_row, k_row, q_col, k_col, out_grad, v_row)

    def load(n):
        return pltpu.make_async_copy(arrays[n], stage.at[n % 2], load_sem.at[n % 2])

    def pack_next(n):
        load(n).wait()
        pack(stage.at[n % 2], sends.at[n])
        if n + 2 < 6:
            load(n + 2).start()

    load(0).start()
    load(1).start()
    loop(6, lambda i: greet(dev(x, y, (z + 1 + i // 2) % 4, i % 2)))
    loop(31, lambda i: greet(plane_dest(i + 1)[0]))
    loop(32, lambda i: greet(col_dest(i)))
    loop(32, lambda i: greet(col_home(i)[0]))
    pack_next(0)
    pack_next(1)
    pack_next(2)
    pl.semaphore_wait(barrier, 101 - jnp.where(home_mine, 2, 0))

    def send_rows(n, dst):
        def body(i):
            z_ = (z + i) % 4
            push(sends.at[n, z_], dst.at[:, pl.ds(pl.multiple_of(g * 128, 128), 128), :],
                 in_send.at[n], in_recv.at[n], row_dest(i))

        loop(4, body)

    def send_plane(n, dst):
        def body(i):
            x_, half, core_ = (x + i) % 4, (y + i // 4) % 2, (core + i // 8) % 2
            push(sends.at[n, pl.ds(2 * core_, 2), :, pl.ds(pl.multiple_of((half * 4 + x_) * 16, 16), 16), :],
                 dst.at[:, chip], in_send.at[n], in_recv.at[n], dev(x_, 2 * core + half, z, core_))

        loop(16, body)

    def send_line(n, src, dst):
        def body(i):
            j = (i + zl) % 2
            push(src.at[j], dst.at[zl], on_send.at[n], on_recv.at[n], dev(x, y, 2 * core + j, zh))

        loop(2, body)

    def wait_in(n):
        if n in (0, 1, 5):
            wait_sent(in_send.at[n], lambda k: sends.at[n, 0:k], 4, row_mine)
        else:
            wait_sent(in_send.at[n], lambda k: mq.at[:, 0:k], 16, plane_mine)

    own_rows = pl.ds(pl.multiple_of(core * 256, 256), 256)
    other_rows = pl.ds(pl.multiple_of((1 - core) * 256, 256), 256)
    own_slab = pl.ds(pl.multiple_of(slab * 16, 16), 16)
    other_core = dev(x, y, z, 1 - core)

    def send_sum(src, dst, n):
        def body(i):
            dest, x_, y_, _ = plane_dest(i)
            push(src(y_ * 4 + x_), dst.at[chip], plane_send.at[n], plane_recv.at[n], dest)

        loop(16, body)

    def share(value, dst, n):
        dst[:, own_slab, :] = value.astype(BF16)
        loop(15, lambda i: push(dst.at[:, own_slab, :], dst.at[:, own_slab, :], plane_send.at[n], plane_recv.at[n],
                                plane_dest(i + 1)[0], False))

    def share_core(dst, n, core_n):
        wait_for(dst.at[:, 0:240, :], plane_recv.at[n])
        push(dst.at[:, own_rows, :], dst.at[:, own_rows, :], core_send.at[core_n], core_recv.at[core_n], other_core, False)
        wait_for(dst.at[:, 0:256, :], core_recv.at[core_n])

    send_rows(0, rq)
    send_rows(1, rk)
    send_plane(2, mq)
    pack_next(3)
    send_plane(3, mk)
    pack_next(4)
    pack_next(5)
    wait_in(0)
    send_rows(5, rv)
    wait_in(2)
    send_plane(4, mo)

    wait_for(rq, in_recv.at[0])
    wait_for(rk, in_recv.at[1])
    row_products(rq, rk, part)
    push(part.at[:, other_rows, :], core_l, core_send.at[0], core_recv.at[0], other_core, False)
    wait_for(mq, in_recv.at[2])
    send_line(0, mq, cq)
    wait_for(core_l, core_recv.at[0])
    part[:, own_rows, :] += core_l[...]
    send_sum(lambda n: part.at[:, pl.ds(pl.multiple_of(core * 256 + n * 16, 16), 16), :], sum_l, 0)
    wait_for(mk, in_recv.at[3])
    send_line(1, mk, ck)
    wait_for(sum_l, plane_recv.at[0])
    logits = sum_l[0]
    for n in range(1, 16):
        logits += sum_l[n]
    logits = logits * ROW_SCALE
    weights = jnp.exp(logits - jnp.max(logits, axis=-1, keepdims=True))
    probs = weights / jnp.sum(weights, axis=-1, keepdims=True)
    tied_f[...] = probs
    share(probs, tied, 1)
    wait_for(mo, in_recv.at[4])
    send_line(2, mo, co)
    share_core(tied, 1, 1)

    wait_for(rv, in_recv.at[5])
    wait_in(5)
    ro = sends.at[5]

    def put_ro(r2, tile, value):
        for b in range(4):
            ro[r2, b, :, tile * 128 : tile * 128 + 128] = value[128 * b : 128 * b + 128]

    row_apply(tied, rv, put_ro, NN)

    def send_ro(i):
        dest, x_, y_, core_ = plane_dest(i)
        t = core_ * 16 + y_ * 4 + x_
        push(ro.at[:, t // 8, pl.ds(pl.multiple_of((t % 8) * 16, 16), 16), :], cro.at[core, chip],
             plane_send.at[2], plane_recv.at[2], dest)

    loop(32, send_ro)

    for n in (1, 3, 4):
        wait_in(n)
    wait_for(cq, on_recv.at[0])
    by_column(cq, wide0, col_q)
    wait_for(ck, on_recv.at[1])
    by_column(ck, wide0, col_k)

    def put_probs(c, h, value):
        for half in range(2):
            rows = value[128 * half : 128 * half + 128]
            if h == 0:
                sends[c // 4, c % 4, half, :, 0:256] = rows
            elif h == 1:
                sends[c // 4, c % 4, half, :, 256:384] = rows[:, 0:128]
                sends[c // 4, c % 4, 2 + half, :, 0:128] = rows[:, 128:256]
            else:
                sends[c // 4, c % 4, 2 + half, :, 128:384] = rows

    def get_probs(c, h):
        rows = []
        for half in range(2):
            if h == 0:
                rows.append(sends[c // 4, c % 4, half, :, 0:256])
            elif h == 1:
                rows.append(jnp.concatenate([sends[c // 4, c % 4, half, :, 256:384], sends[c // 4, c % 4, 2 + half, :, 0:128]], axis=1))
            else:
                rows.append(sends[c // 4, c % 4, 2 + half, :, 128:384])
        return jnp.concatenate(rows, axis=0)

    def probs_pass(c):
        logs = []
        for h, (rows, low) in enumerate(HEADS):
            scores = dot(rows(col_k, c), keep(rows(col_q, c), low), NT) * COL_SCALE
            top = jnp.max(scores, axis=0, keepdims=True)
            weights = jnp.exp(scores - top)
            total = jnp.sum(weights, axis=0, keepdims=True)
            put_probs(c, h, (weights * (1.0 / total)).astype(BF16))
            logs.append(top + jnp.log(total))
        norms[c] = jnp.concatenate(logs, axis=0)

    loop(16, probs_pass)

    wait_for(co, on_recv.at[2])
    by_column(co, wide0, col_o)

    def mixed_pass(c):
        outer = outer_rows(col_o, c)
        put_outer(wide1, c, dot(get_probs(c, 0), outer, NN), dot(get_probs(c, 1), outer, NN))
        put_mid(wide1, c, dot(get_probs(c, 2), mid_rows(col_o, c), NN))

    loop(16, mixed_pass)
    by_row(wide1, cq, (0, 1, 2))

    def send_mixed(i):
        dest, x_, y_, core_ = plane_dest(i)
        push(cq.at[core_, y_ * 4 + x_], rmix.at[:, own_slab, :], plane_send.at[3], plane_recv.at[3], dest)

    loop(32, send_mixed)

    wait_for(cro, plane_recv.at[2])
    by_column(cro, wide0, col_r)

    def slope_parts(c, h):
        rows, low = HEADS[h]
        queries, keys = rows(col_q, c), rows(col_k, c)
        scores = dot(keys, keep(queries, low), NT) * COL_SCALE
        probs = jnp.exp(scores - norms[c, h : h + 1, :])
        grads = dot(rows(col_r, c), keep(rows(col_o, c), low), NT)
        slope = probs * (grads - jnp.sum(probs * grads, axis=0, keepdims=True))
        slope = slope.astype(BF16)
        return dot(slope, keys, TN) * COL_SCALE, dot(slope, queries, NN) * COL_SCALE

    def mid_pass(c):
        q_part, k_part = slope_parts(c, 2)
        put_mid(wide0, c, q_part)
        put_mid(wide1, c, k_part)

    def outer_pass(c):
        q_p, k_p = slope_parts(c, 0)
        q_q, k_q = slope_parts(c, 1)
        put_outer(wide0, c, q_p, q_q)
        put_outer(wide1, c, k_p, k_q)

    def send_home(src, dst, n, lanes):
        def body(i):
            dest, j = col_home(i)
            push(src.at[j % 2, j // 2, :, :, lanes],
                 dst.at[z, :, pl.ds(pl.multiple_of((slab % 8) * 16, 16), 16), lanes],
                 out_send.at[n], out_recv.at[n], dest)

        loop(32, body)

    mid, outer = pl.ds(256, 128), pl.ds(0, 256)
    loop(16, mid_pass)
    by_row(wide0, ck, (2,))
    by_row(wide1, co, (2,))
    send_home(ck, o_qc, 5, mid)
    send_home(co, o_kc, 6, mid)
    loop(16, outer_pass)
    by_row(wide0, ck, (0, 1))
    by_row(wide1, co, (0, 1))
    send_home(ck, o_qc, 3, outer)
    send_home(co, o_kc, 4, outer)

    wait_for(rmix, plane_recv.at[3])
    wait_for(part.at[:, 0:256, :], core_send.at[0])
    wait_for(sum_l.at[0:15], plane_send.at[0])
    row_products(rmix, rv, part)
    push(part.at[:, other_rows, :], core_g, core_send.at[2], core_recv.at[2], other_core, False)

    def in_place(ref):
        def store(r2, tile, value):
            ref[r2, :, tile * 128 : tile * 128 + 128] = value

        return store

    def send_rows_home(src, dst, n):
        def body(i):
            dest, b = row_home(i)
            push(src.at[:, pl.ds(pl.multiple_of(b * 128, 128), 128), :], dst.at[z], out_send.at[n], out_recv.at[n], dest)

        loop(4, body)

    row_apply(tied, rmix, in_place(rmix), TN)
    wait_for(core_g, core_recv.at[2])
    half_g[...] = (part[:, own_rows, :] + core_g[...]).astype(BF16)
    send_sum(lambda n: half_g.at[:, pl.ds(pl.multiple_of(n * 16, 16), 16), :], sum_g, 4)
    send_rows_home(rmix, o_vr, 2)
    wait_for(sum_g, plane_recv.at[4])
    grads = sum_g[0].astype(F32)
    for n in range(1, 16):
        grads += sum_g[n].astype(F32)
    probs = tied_f[...]
    share(probs * (grads - jnp.sum(probs * grads, axis=-1, keepdims=True)), slopes, 5)
    share_core(slopes, 5, 3)

    row_apply(slopes, rk, in_place(rk), NN, ROW_SCALE)
    send_rows_home(rk, o_qr, 0)
    row_apply(slopes, rq, in_place(rq), TN, ROW_SCALE)
    send_rows_home(rq, o_kr, 1)

    for n in range(3):
        wait_sent(on_send.at[n], lambda k: mq.at[0:k], 2, line_mine)
    wait_for(tied.at[:, 0:240, :], plane_send.at[1])
    wait_for(rq.at[:, 0:496, :], plane_send.at[2])
    wait_for(rq.at[:, 0:496, :], plane_send.at[3])
    wait_for(sum_g.at[0:15], plane_send.at[4])
    wait_for(tied.at[:, 0:240, :], plane_send.at[5])
    wait_for(tied.at[:, 0:256, :], core_send.at[1])
    wait_for(core_g, core_send.at[2])
    wait_for(tied.at[:, 0:256, :], core_send.at[3])
    for n, ref in enumerate((o_qr, o_kr, o_vr)):
        wait_sent(out_send.at[n], lambda k: sends.at[0, 0:k], 4, row_mine)
        wait_for(ref, out_recv.at[n])
    for n, ref, lanes in ((5, o_qc, mid), (6, o_kc, mid), (3, o_qc, outer), (4, o_kc, outer)):
        wait_sent(out_send.at[n], lambda k: rq.at[:, 0 : 16 * k, lanes], 32, home_mine)
        wait_for(ref.at[:, :, :, lanes], out_recv.at[n])


def on_device(q_row, k_row, v_row, q_col, k_col, out_grad):
    vm = pltpu.VMEM
    dma = pltpu.SemaphoreType.DMA
    rows, cols = (4, 512, 384), (2, 16, 4, 16, 384)
    packed = pl.pallas_call(
        main_kernel,
        name="layer",
        out_shape=[jax.ShapeDtypeStruct((4, 4, 128, 384), BF16)] * 5,
        in_specs=[pl.BlockSpec(memory_space=pl.ANY)] * 6,
        out_specs=[pl.BlockSpec(memory_space=pl.ANY)] * 5,
        scratch_shapes=[
            vm((2, 8, 128, 768), BF16),
            vm((6, 4, 4, 128, 384), BF16),
            vm(rows, BF16), vm(rows, BF16), vm(rows, BF16),
            vm(cols, BF16), vm(cols, BF16), vm(cols, BF16),
            vm(cols, BF16), vm(cols, BF16), vm(cols, BF16), vm(cols, BF16),
            vm(rows, BF16),
            vm((3, 512, 512), F32),
            vm((3, 256, 512), F32), vm((3, 256, 512), F32),
            vm((16, 3, 16, 512), F32),
            vm((3, 256, 512), BF16),
            vm((16, 3, 16, 512), BF16),
            vm((3, 16, 512), F32),
            vm((3, 512, 512), BF16), vm((3, 512, 512), BF16),
            vm((3, 2048, 128), F32), vm((3, 2048, 128), F32),
            vm((16, 128, 384), BF16), vm((16, 128, 384), BF16), vm((16, 128, 384), BF16), vm((16, 128, 384), BF16),
            vm((16, 3, 256), F32),
            dma((2,)), dma((6,)), dma((6,)), dma((3,)), dma((3,)), dma((6,)), dma((6,)), dma((4,)), dma((4,)),
            dma((7,)), dma((7,)),
        ],
        compiler_params=pltpu.CompilerParams(collective_id=0, has_side_effects=True, vmem_limit_bytes=62 << 20),
    )(q_row, k_row, v_row, q_col, k_col, out_grad)
    return unpack(packed)


def solution(mesh):
    spec = P("seq", "col", None)
    return jax.shard_map(on_device, mesh=mesh, in_specs=(spec,) * 6, out_specs=(spec,) * 5, check_vma=False)
```

```python
import math

import jax
import jax.numpy as jnp
from jax import lax
from jax.experimental import pallas as pl
from jax.experimental.pallas import tpu as pltpu
from jax.sharding import PartitionSpec as P

MESH = pl.DeviceIdType.MESH
F32 = jnp.float32
BF16 = jnp.bfloat16
NT = (((1,), (1,)), ((), ()))
NN = (((1,), (0,)), ((), ()))
TN = (((0,), (0,)), ((), ()))
ROW_SCALE = 1.0 / math.sqrt(16384.0)
COL_SCALE = 1.0 / math.sqrt(64.0)


def dot(a, b, dims):
    return lax.dot_general(a, b, dims, preferred_element_type=F32)


def swap_halves(t):
    return jnp.concatenate([t[..., 64:128], t[..., 0:64]], axis=-1)


def low_lanes(shape):
    return lax.broadcasted_iota(jnp.int32, shape, len(shape) - 1) % 128 < 64


def pack(src, dst):
    lo = low_lanes((128, 128))

    def step(r2, _):
        for half in range(2):
            base = half * 384
            mid_a, mid_b = src[r2, :, base + 128 : base + 256], src[r2 + 4, :, base + 128 : base + 256]
            turned = swap_halves(mid_b)
            even, odd = 2 * half, 2 * half + 1
            dst[even, r2, :, 0:128] = src[r2, :, base : base + 128]
            dst[even, r2, :, 128:256] = src[r2 + 4, :, base : base + 128]
            dst[even, r2, :, 256:384] = jnp.where(lo, mid_a, turned)
            dst[odd, r2, :, 0:128] = src[r2, :, base + 256 : base + 384]
            dst[odd, r2, :, 128:256] = src[r2 + 4, :, base + 256 : base + 384]
            dst[odd, r2, :, 256:384] = jnp.where(lo, turned, mid_a)
        return 0

    lax.fori_loop(0, 4, step, 0)


def unpack_kernel(*refs):
    lo = low_lanes((128, 128))
    for src, dst in zip(refs[:5], refs[5:]):
        for half, k in ((0, 0), (0, 1), (1, 0), (1, 1)):
            base = half * 384
            even, odd = 2 * half, 2 * half + 1
            mid_even, mid_odd = src[even, k, :, 256:384], src[odd, k, :, 256:384]
            dst[0, k, :, base : base + 128] = src[even, k, :, 0:128]
            dst[1, k, :, base : base + 128] = src[even, k, :, 128:256]
            dst[0, k, :, base + 128 : base + 256] = jnp.where(lo, mid_even, mid_odd)
            dst[1, k, :, base + 128 : base + 256] = swap_halves(jnp.where(lo, mid_odd, mid_even))
            dst[0, k, :, base + 256 : base + 384] = src[odd, k, :, 0:128]
            dst[1, k, :, base + 256 : base + 384] = src[odd, k, :, 128:256]


def unpack(packed):
    outs = pl.pallas_call(
        unpack_kernel,
        name="unpack",
        grid=(2,),
        out_shape=[jax.ShapeDtypeStruct((2, 4, 128, 768), BF16)] * 5,
        in_specs=[pl.BlockSpec((4, 2, 128, 384), lambda i: (0, i, 0, 0))] * 5,
        out_specs=[pl.BlockSpec((2, 2, 128, 768), lambda i: (0, i, 0, 0))] * 5,
        compiler_params=pltpu.CompilerParams(vmem_limit_bytes=62 << 20),
    )(*packed)
    return tuple(o.reshape(8, 128, 768) for o in outs)


def row_product(a, b, out, h):
    low = low_lanes((512, 512))
    zero = jnp.zeros((512, 512), BF16)
    total = None
    if h < 2:
        for u in (0, 2):
            left = jnp.concatenate([a[u, :, 0:256], a[u + 1, :, 0:256]], axis=1)
            right = jnp.concatenate([b[u, :, 0:256], b[u + 1, :, 0:256]], axis=1)
            left = jnp.where(low, left, zero) if h == 0 else jnp.where(low, zero, left)
            term = dot(left, right, NT)
            total = term if total is None else total + term
    else:
        left = jnp.concatenate([a[u, :, 256:384] for u in range(4)], axis=1)
        right = jnp.concatenate([b[u, :, 256:384] for u in range(4)], axis=1)
        total = dot(left, right, NT)
    out[h] = total


def row_apply(m, b, store, dims, scale=None):
    low = low_lanes((512, 256))

    def step(pair, _):
        for r2 in (2 * pair, 2 * pair + 1):
            right = b[r2, :, 0:256]
            both = jnp.where(low, dot(m[0], right, dims), dot(m[1], right, dims))
            if scale is not None:
                both = both * scale
            both = both.astype(BF16)
            store(r2, 0, both[:, 0:128])
            store(r2, 1, both[:, 128:256])
        right = jnp.concatenate([b[2 * pair, :, 256:384], b[2 * pair + 1, :, 256:384]], axis=1)
        third = dot(m[2], right, dims)
        if scale is not None:
            third = third * scale
        third = third.astype(BF16)
        store(2 * pair, 2, third[:, 0:128])
        store(2 * pair + 1, 2, third[:, 128:256])
        return 0

    lax.fori_loop(0, 2, step, 0)


def by_column(src, wide, dst):
    def widen(i, _):
        block = src[i // 4, pl.ds((i % 4) * 4, 4)].reshape(256, 384).astype(F32)
        for t in range(3):
            wide[t, pl.ds(pl.multiple_of(i * 256, 256), 256), :] = block[:, 128 * t : 128 * t + 128]
        return 0

    lax.fori_loop(0, 8, widen, 0)

    def gather(c, _):
        rows = pl.ds(c, 128, stride=16)
        mid = wide[2, rows, :]
        dst[c, 0:128, 0:128] = wide[0, rows, :].astype(BF16)
        dst[c, 128:256, 0:128] = wide[1, rows, :].astype(BF16)
        dst[c, 0:128, 128:256] = mid.astype(BF16)
        dst[c, 128:256, 128:256] = pltpu.roll(mid, 64, 1).astype(BF16)
        return 0

    lax.fori_loop(0, 16, gather, 0)


def by_row(wide, dst, tiles):
    def narrow(i, _):
        for t in tiles:
            block = wide[t, pl.ds(pl.multiple_of(i * 256, 256), 256), :].astype(BF16)
            dst[i // 4, pl.ds((i % 4) * 4, 4), :, :, 128 * t : 128 * t + 128] = block.reshape(4, 4, 16, 128)
        return 0

    lax.fori_loop(0, 8, narrow, 0)


def outer_rows(ref, c):
    return ref[c, :, 0:128]


def mid_rows(ref, c):
    return ref[c, :, 128:256]


def keep(x, low):
    lo = low_lanes(x.shape)
    zero = jnp.zeros_like(x)
    return jnp.where(lo, x, zero) if low else jnp.where(lo, zero, x)


HEADS = ((outer_rows, True), (outer_rows, False), (mid_rows, True))


def put_outer(wide, c, p_part, q_part):
    outer = jnp.where(low_lanes((256, 128)), p_part, q_part)
    rows = pl.ds(c, 128, stride=16)
    wide[0, rows, :] = outer[0:128]
    wide[1, rows, :] = outer[128:256]


def put_mid(wide, c, part):
    wide[2, pl.ds(c, 128, stride=16), :] = jnp.where(low_lanes((128, 128)), part[0:128], pltpu.roll(part[128:256], 64, 1))


def main_kernel(
    q_row, k_row, v_row, q_col, k_col, out_grad,
    o_qr, o_kr, o_vr, o_qc, o_kc,
    stage, sends, rq, rk, rv, mq, mk, mo, cq, ck, co, cro, rmix,
    part, core_l, core_g, sum_l, half_g, sum_g, tied_f, tied, slopes,
    wide0, wide1, col_q, col_k, col_o, col_r, norms,
    load_sem, in_send, in_recv, on_send, on_recv, plane_send, plane_recv, core_send, core_recv, out_send, out_recv,
):
    s, g = lax.axis_index("seq"), lax.axis_index("col")
    x, y, zl = (s // 2) % 4, s // 8, s % 2
    zh, core = g // 2, g % 2
    z = 2 * zh + zl
    chip = y * 4 + x
    slab = core * 16 + chip

    def dev(x_, y_, z_, core_):
        return (y_ * 8 + x_ * 2 + z_ % 2, (z_ // 2) * 2 + core_)

    def is_me(d):
        return jnp.logical_and(d[0] == s, d[1] == g)

    def push(src, dst, send_sem, recv_sem, dest, maybe_me=True):
        def remote():
            pltpu.make_async_remote_copy(
                src_ref=src, dst_ref=dst, send_sem=send_sem, recv_sem=recv_sem, device_id=dest, device_id_type=MESH
            ).start()

        if not maybe_me:
            remote()
            return
        me = is_me(dest)
        pl.when(jnp.logical_not(me))(remote)

        @pl.when(me)
        def _():
            pltpu.make_async_copy(src, dst, recv_sem).start()

    def wait_for(ref, sem):
        pltpu.make_async_copy(ref, ref, sem).wait()

    def wait_sent(sem, chunks, count, mine):
        @pl.when(mine)
        def _():
            wait_for(chunks(count - 1), sem)

        @pl.when(jnp.logical_not(mine))
        def _():
            wait_for(chunks(count), sem)

    def loop(n, body):
        def step(i, _):
            body(i)
            return 0

        lax.fori_loop(0, n, step, 0)

    def columns(body):
        def four(i):
            for j in range(4):
                body(4 * i + j)

        loop(4, four)

    row_mine = core == zl
    plane_mine = y // 2 == core
    line_mine = core == zh
    home_mine = jnp.logical_and(line_mine, plane_mine)

    def row_dest(i):
        return dev(x, y, (z + i) % 4, zl)

    def row_home(i):
        return dev(x, y, 2 * (i // 2) + core, i % 2), i

    def col_dest(i):
        m = (i // 4 + s) % 8
        return dev(m % 4, 2 * core + m // 4, (z + i) % 4, zh)

    def col_home(i):
        j = (s + i) % 32
        return (j, core * 2 + y // 2), j

    def plane_dest(i):
        x_, y_, core_ = (x + i) % 4, (y + (i // 4)) % 4, (core + i // 16) % 2
        return dev(x_, y_, z, core_), x_, y_, core_

    barrier = pltpu.get_barrier_semaphore()

    def greet(dest):
        @pl.when(jnp.logical_not(is_me(dest)))
        def _():
            pl.semaphore_signal(barrier, inc=1, device_id=dest, device_id_type=MESH)

    arrays = (q_row, k_row, q_col, k_col, out_grad, v_row)

    def load(n):
        return pltpu.make_async_copy(arrays[n], stage.at[n % 2], load_sem.at[n % 2])

    def pack_next(n):
        load(n).wait()
        pack(stage.at[n % 2], sends.at[n])
        if n + 2 < 6:
            load(n + 2).start()

    load(0).start()
    load(1).start()
    loop(6, lambda i: greet(dev(x, y, (z + 1 + i // 2) % 4, i % 2)))
    loop(31, lambda i: greet(plane_dest(i + 1)[0]))
    loop(32, lambda i: greet(col_dest(i)))
    loop(32, lambda i: greet(col_home(i)[0]))
    pack_next(0)
    pack_next(1)
    pack_next(2)
    pl.semaphore_wait(barrier, 101 - jnp.where(home_mine, 2, 0))

    def send_rows(n, dst):
        def body(i):
            z_ = (z + i) % 4
            push(sends.at[n, z_], dst.at[:, pl.ds(pl.multiple_of(g * 128, 128), 128), :],
                 in_send.at[n], in_recv.at[n], row_dest(i))

        loop(4, body)

    def send_plane(n, dst):
        def body(i):
            x_, half, core_ = (x + i) % 4, (y + i // 4) % 2, (core + i // 8) % 2
            push(sends.at[n, pl.ds(2 * core_, 2), :, pl.ds(pl.multiple_of((half * 4 + x_) * 16, 16), 16), :],
                 dst.at[:, chip], in_send.at[n], in_recv.at[n], dev(x_, 2 * core + half, z, core_))

        loop(16, body)

    def send_line(n, src, dst):
        def body(i):
            j = (i + zl) % 2
            push(src.at[j], dst.at[zl], on_send.at[n], on_recv.at[n], dev(x, y, 2 * core + j, zh))

        loop(2, body)

    def wait_in(n):
        if n in (0, 1, 5):
            wait_sent(in_send.at[n], lambda k: sends.at[n, 0:k], 4, row_mine)
        else:
            wait_sent(in_send.at[n], lambda k: mq.at[:, 0:k], 16, plane_mine)

    own_rows = pl.ds(pl.multiple_of(core * 256, 256), 256)
    other_rows = pl.ds(pl.multiple_of((1 - core) * 256, 256), 256)
    own_slab = pl.ds(pl.multiple_of(slab * 16, 16), 16)
    other_core = dev(x, y, z, 1 - core)

    def send_sum(src, dst, n):
        def body(i):
            dest, x_, y_, _ = plane_dest(i)
            push(src(y_ * 4 + x_), dst.at[chip], plane_send.at[n], plane_recv.at[n], dest)

        loop(16, body)

    def share(value, dst, n):
        dst[own_slab, :] = value.astype(BF16)
        loop(15, lambda i: push(dst.at[own_slab, :], dst.at[own_slab, :], plane_send.at[n], plane_recv.at[n],
                                plane_dest(i + 1)[0], False))

    def share_core(dst, n, core_n):
        for h in range(3):
            wait_for(dst.at[h, 0:240, :], plane_recv.at[n + h])
            push(dst.at[h, own_rows, :], dst.at[h, own_rows, :], core_send.at[core_n + h], core_recv.at[core_n + h],
                 other_core, False)
        for h in range(3):
            wait_for(dst.at[h, 0:256, :], core_recv.at[core_n + h])

    def products(a, b, inbox, core_n):
        for h in range(3):
            row_product(a, b, part, h)
            push(part.at[h, other_rows, :], inbox.at[h], core_send.at[core_n + h], core_recv.at[core_n + h], other_core, False)

    def add_up(ref):
        total = ref[0].astype(F32)
        for n in range(1, 16):
            total += ref[n].astype(F32)
        return total

    send_rows(0, rq)
    send_rows(1, rk)
    send_plane(2, mq)
    pack_next(3)
    send_plane(3, mk)
    pack_next(4)
    pack_next(5)
    wait_in(0)
    send_rows(5, rv)
    wait_in(2)
    send_plane(4, mo)

    wait_for(rq, in_recv.at[0])
    wait_for(rk, in_recv.at[1])
    products(rq, rk, core_l, 0)
    wait_for(mq, in_recv.at[2])
    send_line(0, mq, cq)
    for h in range(3):
        wait_for(core_l.at[h], core_recv.at[h])
        part[h, own_rows, :] += core_l[h]
        send_sum(lambda n: part.at[h, pl.ds(pl.multiple_of(core * 256 + n * 16, 16), 16), :], sum_l.at[h], h)
    wait_for(mk, in_recv.at[3])
    send_line(1, mk, ck)
    for h in range(3):
        wait_for(sum_l.at[h], plane_recv.at[h])
        logits = add_up(sum_l.at[h]) * ROW_SCALE
        weights = jnp.exp(logits - jnp.max(logits, axis=-1, keepdims=True))
        probs = weights / jnp.sum(weights, axis=-1, keepdims=True)
        tied_f[h] = probs
        share(probs, tied.at[h], 3 + h)
    wait_for(mo, in_recv.at[4])
    send_line(2, mo, co)
    share_core(tied, 3, 3)

    wait_for(rv, in_recv.at[5])
    wait_in(5)
    ro = sends.at[5]

    def put_ro(r2, tile, value):
        for b in range(4):
            ro[r2, b, :, tile * 128 : tile * 128 + 128] = value[128 * b : 128 * b + 128]

    row_apply(tied, rv, put_ro, NN)

    def send_ro(i):
        dest, x_, y_, core_ = plane_dest(i)
        t = core_ * 16 + y_ * 4 + x_
        push(ro.at[:, t // 8, pl.ds(pl.multiple_of((t % 8) * 16, 16), 16), :], cro.at[core, chip],
             plane_send.at[6], plane_recv.at[6], dest)

    loop(32, send_ro)

    for n in (1, 3, 4):
        wait_in(n)
    wait_for(cq, on_recv.at[0])
    by_column(cq, wide0, col_q)
    wait_for(ck, on_recv.at[1])
    by_column(ck, wide0, col_k)

    def put_probs(c, h, value):
        for half in range(2):
            rows = value[128 * half : 128 * half + 128]
            if h == 0:
                sends[c // 4, c % 4, half, :, 0:256] = rows
            elif h == 1:
                sends[c // 4, c % 4, half, :, 256:384] = rows[:, 0:128]
                sends[c // 4, c % 4, 2 + half, :, 0:128] = rows[:, 128:256]
            else:
                sends[c // 4, c % 4, 2 + half, :, 128:384] = rows

    def get_probs(c, h):
        rows = []
        for half in range(2):
            if h == 0:
                rows.append(sends[c // 4, c % 4, half, :, 0:256])
            elif h == 1:
                rows.append(jnp.concatenate([sends[c // 4, c % 4, half, :, 256:384], sends[c // 4, c % 4, 2 + half, :, 0:128]], axis=1))
            else:
                rows.append(sends[c // 4, c % 4, 2 + half, :, 128:384])
        return jnp.concatenate(rows, axis=0)

    def probs_pass(c):
        logs = []
        for h, (rows, low) in enumerate(HEADS):
            scores = dot(rows(col_k, c), keep(rows(col_q, c), low), NT) * COL_SCALE
            top = jnp.max(scores, axis=0, keepdims=True)
            weights = jnp.exp(scores - top)
            total = jnp.sum(weights, axis=0, keepdims=True)
            put_probs(c, h, (weights * (1.0 / total)).astype(BF16))
            logs.append(top + jnp.log(total))
        norms[c] = jnp.concatenate(logs, axis=0)

    columns(probs_pass)

    wait_for(co, on_recv.at[2])
    by_column(co, wide0, col_o)

    def mixed_pass(c):
        outer = outer_rows(col_o, c)
        put_outer(wide1, c, dot(get_probs(c, 0), outer, NN), dot(get_probs(c, 1), outer, NN))
        put_mid(wide1, c, dot(get_probs(c, 2), mid_rows(col_o, c), NN))

    columns(mixed_pass)
    by_row(wide1, cq, (0, 1, 2))

    def send_mixed(i):
        dest, x_, y_, core_ = plane_dest(i)
        push(cq.at[core_, y_ * 4 + x_], rmix.at[:, own_slab, :], plane_send.at[7], plane_recv.at[7], dest)

    loop(32, send_mixed)

    wait_for(cro, plane_recv.at[6])
    by_column(cro, wide0, col_r)

    def slope_parts(c, h):
        rows, low = HEADS[h]
        queries, keys = rows(col_q, c), rows(col_k, c)
        scores = dot(keys, keep(queries, low), NT) * COL_SCALE
        probs = jnp.exp(scores - norms[c, h : h + 1, :])
        grads = dot(rows(col_r, c), keep(rows(col_o, c), low), NT)
        slope = probs * (grads - jnp.sum(probs * grads, axis=0, keepdims=True))
        slope = slope.astype(BF16)
        return dot(slope, keys, TN) * COL_SCALE, dot(slope, queries, NN) * COL_SCALE

    def mid_pass(c):
        q_part, k_part = slope_parts(c, 2)
        put_mid(wide0, c, q_part)
        put_mid(wide1, c, k_part)

    def outer_pass(c):
        q_p, k_p = slope_parts(c, 0)
        q_q, k_q = slope_parts(c, 1)
        put_outer(wide0, c, q_p, q_q)
        put_outer(wide1, c, k_p, k_q)

    def send_home(src, dst, n, lanes):
        def body(i):
            dest, j = col_home(i)
            push(src.at[j % 2, j // 2, :, :, lanes],
                 dst.at[z, :, pl.ds(pl.multiple_of((slab % 8) * 16, 16), 16), lanes],
                 out_send.at[n], out_recv.at[n], dest)

        loop(32, body)

    mid, outer = pl.ds(256, 128), pl.ds(0, 256)
    columns(mid_pass)
    by_row(wide0, ck, (2,))
    by_row(wide1, co, (2,))
    send_home(ck, o_qc, 5, mid)
    send_home(co, o_kc, 6, mid)
    columns(outer_pass)
    by_row(wide0, ck, (0, 1))
    by_row(wide1, co, (0, 1))
    send_home(ck, o_qc, 3, outer)
    send_home(co, o_kc, 4, outer)

    wait_for(rmix, plane_recv.at[7])
    for h in range(3):
        wait_for(part.at[h, 0:256, :], core_send.at[h])
        wait_for(sum_l.at[h, 0:15], plane_send.at[h])
    products(rmix, rv, core_g, 6)

    def in_place(ref):
        def store(r2, tile, value):
            ref[r2, :, tile * 128 : tile * 128 + 128] = value

        return store

    def send_rows_home(src, dst, n):
        def body(i):
            dest, b = row_home(i)
            push(src.at[:, pl.ds(pl.multiple_of(b * 128, 128), 128), :], dst.at[z], out_send.at[n], out_recv.at[n], dest)

        loop(4, body)

    for h in range(3):
        wait_for(core_g.at[h], core_recv.at[6 + h])
        half_g[h] = (part[h, own_rows, :] + core_g[h]).astype(BF16)
        send_sum(lambda n: half_g.at[h, pl.ds(pl.multiple_of(n * 16, 16), 16), :], sum_g.at[h], 8 + h)
    row_apply(tied, rmix, in_place(rmix), TN)
    send_rows_home(rmix, o_vr, 2)
    for h in range(3):
        wait_for(sum_g.at[h], plane_recv.at[8 + h])
        grads = add_up(sum_g.at[h])
        probs = tied_f[h]
        share(probs * (grads - jnp.sum(probs * grads, axis=-1, keepdims=True)), slopes.at[h], 11 + h)
    share_core(slopes, 11, 9)

    row_apply(slopes, rk, in_place(rk), NN, ROW_SCALE)
    send_rows_home(rk, o_qr, 0)
    row_apply(slopes, rq, in_place(rq), TN, ROW_SCALE)
    send_rows_home(rq, o_kr, 1)

    for n in range(3):
        wait_sent(on_send.at[n], lambda k: mq.at[0:k], 2, line_mine)
    wait_for(rq.at[:, 0:496, :], plane_send.at[6])
    wait_for(rq.at[:, 0:496, :], plane_send.at[7])
    for h in range(3):
        wait_for(tied.at[h, 0:240, :], plane_send.at[3 + h])
        wait_for(sum_g.at[h, 0:15], plane_send.at[8 + h])
        wait_for(tied.at[h, 0:240, :], plane_send.at[11 + h])
        wait_for(tied.at[h, 0:256, :], core_send.at[3 + h])
        wait_for(core_g.at[h], core_send.at[6 + h])
        wait_for(tied.at[h, 0:256, :], core_send.at[9 + h])
    for n, ref in enumerate((o_qr, o_kr, o_vr)):
        wait_sent(out_send.at[n], lambda k: sends.at[0, 0:k], 4, row_mine)
        wait_for(ref, out_recv.at[n])
    for n, ref, lanes in ((5, o_qc, mid), (6, o_kc, mid), (3, o_qc, outer), (4, o_kc, outer)):
        wait_sent(out_send.at[n], lambda k: rq.at[:, 0 : 16 * k, lanes], 32, home_mine)
        wait_for(ref.at[:, :, :, lanes], out_recv.at[n])


def on_device(q_row, k_row, v_row, q_col, k_col, out_grad):
    vm = pltpu.VMEM
    dma = pltpu.SemaphoreType.DMA
    rows, cols = (4, 512, 384), (2, 16, 4, 16, 384)
    packed = pl.pallas_call(
        main_kernel,
        name="layer",
        out_shape=[jax.ShapeDtypeStruct((4, 4, 128, 384), BF16)] * 5,
        in_specs=[pl.BlockSpec(memory_space=pl.ANY)] * 6,
        out_specs=[pl.BlockSpec(memory_space=pl.ANY)] * 5,
        scratch_shapes=[
            vm((2, 8, 128, 768), BF16),
            vm((6, 4, 4, 128, 384), BF16),
            vm(rows, BF16), vm(rows, BF16), vm(rows, BF16),
            vm(cols, BF16), vm(cols, BF16), vm(cols, BF16),
            vm(cols, BF16), vm(cols, BF16), vm(cols, BF16), vm(cols, BF16),
            vm(rows, BF16),
            vm((3, 512, 512), F32),
            vm((3, 256, 512), F32), vm((3, 256, 512), F32),
            vm((3, 16, 16, 512), F32),
            vm((3, 256, 512), BF16),
            vm((3, 16, 16, 512), BF16),
            vm((3, 16, 512), F32),
            vm((3, 512, 512), BF16), vm((3, 512, 512), BF16),
            vm((3, 2048, 128), F32), vm((3, 2048, 128), F32),
            vm((16, 256, 256), BF16), vm((16, 256, 256), BF16), vm((16, 256, 256), BF16), vm((16, 256, 256), BF16),
            vm((16, 3, 256), F32),
            dma((2,)), dma((6,)), dma((6,)), dma((3,)), dma((3,)), dma((14,)), dma((14,)), dma((12,)), dma((12,)),
            dma((7,)), dma((7,)),
        ],
        compiler_params=pltpu.CompilerParams(collective_id=0, has_side_effects=True, vmem_limit_bytes=62 << 20),
    )(q_row, k_row, v_row, q_col, k_col, out_grad)
    return unpack(packed)


def solution(mesh):
    spec = P("seq", "col", None)
    return jax.shard_map(on_device, mesh=mesh, in_specs=(spec,) * 6, out_specs=(spec,) * 5, check_vma=False)
```

```python
import math

import jax
import jax.numpy as jnp
from jax import lax
from jax.experimental import pallas as pl
from jax.experimental.pallas import tpu as pltpu
from jax.sharding import PartitionSpec as P

MESH = pl.DeviceIdType.MESH
F32 = jnp.float32
BF16 = jnp.bfloat16
NT = (((1,), (1,)), ((), ()))
NN = (((1,), (0,)), ((), ()))
TN = (((0,), (0,)), ((), ()))
ROW_SCALE = 1.0 / math.sqrt(16384.0)
COL_SCALE = 1.0 / math.sqrt(64.0)


def dot(a, b, dims):
    return lax.dot_general(a, b, dims, preferred_element_type=F32)


def swap_halves(t):
    return jnp.concatenate([t[..., 64:128], t[..., 0:64]], axis=-1)


def low_lanes(shape):
    return lax.broadcasted_iota(jnp.int32, shape, len(shape) - 1) % 128 < 64


def pack(src, dst):
    lo = low_lanes((128, 128))

    def step(r2, _):
        for half in range(2):
            base = half * 384
            mid_a, mid_b = src[r2, :, base + 128 : base + 256], src[r2 + 4, :, base + 128 : base + 256]
            turned = swap_halves(mid_b)
            even, odd = 2 * half, 2 * half + 1
            dst[even, r2, :, 0:128] = src[r2, :, base : base + 128]
            dst[even, r2, :, 128:256] = src[r2 + 4, :, base : base + 128]
            dst[even, r2, :, 256:384] = jnp.where(lo, mid_a, turned)
            dst[odd, r2, :, 0:128] = src[r2, :, base + 256 : base + 384]
            dst[odd, r2, :, 128:256] = src[r2 + 4, :, base + 256 : base + 384]
            dst[odd, r2, :, 256:384] = jnp.where(lo, turned, mid_a)
        return 0

    lax.fori_loop(0, 4, step, 0)


def unpack_kernel(*refs):
    lo = low_lanes((128, 128))
    for src, dst in zip(refs[:5], refs[5:]):
        for half, k in ((0, 0), (0, 1), (1, 0), (1, 1)):
            base = half * 384
            even, odd = 2 * half, 2 * half + 1
            mid_even, mid_odd = src[even, k, :, 256:384], src[odd, k, :, 256:384]
            dst[0, k, :, base : base + 128] = src[even, k, :, 0:128]
            dst[1, k, :, base : base + 128] = src[even, k, :, 128:256]
            dst[0, k, :, base + 128 : base + 256] = jnp.where(lo, mid_even, mid_odd)
            dst[1, k, :, base + 128 : base + 256] = swap_halves(jnp.where(lo, mid_odd, mid_even))
            dst[0, k, :, base + 256 : base + 384] = src[odd, k, :, 0:128]
            dst[1, k, :, base + 256 : base + 384] = src[odd, k, :, 128:256]


def unpack(packed):
    outs = pl.pallas_call(
        unpack_kernel,
        name="unpack",
        grid=(2,),
        out_shape=[jax.ShapeDtypeStruct((2, 4, 128, 768), BF16)] * 5,
        in_specs=[pl.BlockSpec((4, 2, 128, 384), lambda i: (0, i, 0, 0))] * 5,
        out_specs=[pl.BlockSpec((2, 2, 128, 768), lambda i: (0, i, 0, 0))] * 5,
        compiler_params=pltpu.CompilerParams(vmem_limit_bytes=62 << 20),
    )(*packed)
    return tuple(o.reshape(8, 128, 768) for o in outs)


def row_product(a, b, out, h):
    low = low_lanes((512, 512))
    zero = jnp.zeros((512, 512), BF16)
    total = None
    if h < 2:
        for u in (0, 2):
            left = jnp.concatenate([a[u, :, 0:256], a[u + 1, :, 0:256]], axis=1)
            right = jnp.concatenate([b[u, :, 0:256], b[u + 1, :, 0:256]], axis=1)
            left = jnp.where(low, left, zero) if h == 0 else jnp.where(low, zero, left)
            term = dot(left, right, NT)
            total = term if total is None else total + term
    else:
        left = jnp.concatenate([a[u, :, 256:384] for u in range(4)], axis=1)
        right = jnp.concatenate([b[u, :, 256:384] for u in range(4)], axis=1)
        total = dot(left, right, NT)
    out[h] = total


def finish(value, scale):
    return (value if scale is None else value * scale).astype(BF16)


def apply_outer(m, b, store, dims, scale=None):
    low = low_lanes((512, 256))

    def step(pair, _):
        for r2 in (2 * pair, 2 * pair + 1):
            right = b[r2, :, 0:256]
            both = finish(jnp.where(low, dot(m[0], right, dims), dot(m[1], right, dims)), scale)
            store(r2, 0, both[:, 0:128])
            store(r2, 1, both[:, 128:256])
        return 0

    lax.fori_loop(0, 2, step, 0)


def apply_mid(m, b, store, dims, scale=None):
    def step(pair, _):
        right = jnp.concatenate([b[2 * pair, :, 256:384], b[2 * pair + 1, :, 256:384]], axis=1)
        third = finish(dot(m[2], right, dims), scale)
        store(2 * pair, 2, third[:, 0:128])
        store(2 * pair + 1, 2, third[:, 128:256])
        return 0

    lax.fori_loop(0, 2, step, 0)


def row_apply(*args):
    apply_outer(*args)
    apply_mid(*args)


def by_column(src, wide, dst, tiles=(0, 1, 2)):
    def widen(i, _):
        for t in tiles:
            block = src[i // 4, pl.ds((i % 4) * 4, 4), :, :, 128 * t : 128 * t + 128]
            wide[t, pl.ds(pl.multiple_of(i * 256, 256), 256), :] = block.reshape(256, 128).astype(F32)
        return 0

    lax.fori_loop(0, 8, widen, 0)

    def gather(i, _):
        for c in (2 * i, 2 * i + 1):
            rows = pl.ds(c, 128, stride=16)
            for t in tiles:
                if t < 2:
                    dst[c, 128 * t : 128 * t + 128, 0:128] = wide[t, rows, :].astype(BF16)
                else:
                    mid = wide[2, rows, :]
                    dst[c, 0:128, 128:256] = mid.astype(BF16)
                    dst[c, 128:256, 128:256] = pltpu.roll(mid, 64, 1).astype(BF16)
        return 0

    lax.fori_loop(0, 8, gather, 0)


def by_row(wide, dst, tiles):
    def narrow(i, _):
        for t in tiles:
            block = wide[t, pl.ds(pl.multiple_of(i * 256, 256), 256), :].astype(BF16)
            dst[i // 4, pl.ds((i % 4) * 4, 4), :, :, 128 * t : 128 * t + 128] = block.reshape(4, 4, 16, 128)
        return 0

    lax.fori_loop(0, 8, narrow, 0)


def outer_rows(ref, c):
    return ref[c, :, 0:128]


def mid_rows(ref, c):
    return ref[c, :, 128:256]


def keep(x, low):
    lo = low_lanes(x.shape)
    zero = jnp.zeros_like(x)
    return jnp.where(lo, x, zero) if low else jnp.where(lo, zero, x)


HEADS = ((outer_rows, True), (outer_rows, False), (mid_rows, True))


def put_outer(wide, c, p_part, q_part):
    outer = jnp.where(low_lanes((256, 128)), p_part, q_part)
    rows = pl.ds(c, 128, stride=16)
    wide[0, rows, :] = outer[0:128]
    wide[1, rows, :] = outer[128:256]


def put_mid(wide, c, part):
    wide[2, pl.ds(c, 128, stride=16), :] = jnp.where(low_lanes((128, 128)), part[0:128], pltpu.roll(part[128:256], 64, 1))


def main_kernel(
    q_row, k_row, v_row, q_col, k_col, out_grad,
    o_qr, o_kr, o_vr, o_qc, o_kc,
    stage, sends, rq, rk, rv, mq, mk, mo, cq, ck, co, cro, rmix,
    part, core_l, core_g, sum_l, half_g, sum_g, tied_f, tied, slopes,
    wide0, wide1, col_q, col_k, col_o, col_r, norms,
    load_sem, in_send, in_recv, on_send, on_recv, plane_send, plane_recv, core_send, core_recv, out_send, out_recv,
):
    s, g = lax.axis_index("seq"), lax.axis_index("col")
    x, y, zl = (s // 2) % 4, s // 8, s % 2
    zh, core = g // 2, g % 2
    z = 2 * zh + zl
    chip = y * 4 + x
    slab = core * 16 + chip

    def dev(x_, y_, z_, core_):
        return (y_ * 8 + x_ * 2 + z_ % 2, (z_ // 2) * 2 + core_)

    def is_me(d):
        return jnp.logical_and(d[0] == s, d[1] == g)

    def push(src, dst, send_sem, recv_sem, dest, maybe_me=True):
        def remote():
            pltpu.make_async_remote_copy(
                src_ref=src, dst_ref=dst, send_sem=send_sem, recv_sem=recv_sem, device_id=dest, device_id_type=MESH
            ).start()

        if not maybe_me:
            remote()
            return
        me = is_me(dest)
        pl.when(jnp.logical_not(me))(remote)

        @pl.when(me)
        def _():
            pltpu.make_async_copy(src, dst, recv_sem).start()

    def wait_for(ref, sem):
        pltpu.make_async_copy(ref, ref, sem).wait()

    def wait_sent(sem, chunks, count, mine):
        @pl.when(mine)
        def _():
            wait_for(chunks(count - 1), sem)

        @pl.when(jnp.logical_not(mine))
        def _():
            wait_for(chunks(count), sem)

    def loop(n, body):
        def step(i, _):
            body(i)
            return 0

        lax.fori_loop(0, n, step, 0)

    def columns(body):
        def four(i):
            for j in range(4):
                body(4 * i + j)

        loop(4, four)

    def fan(n, body):
        body(0, True)
        loop(n - 1, lambda i: body(i + 1, False))

    row_mine = core == zl
    plane_mine = y // 2 == core
    line_mine = core == zh
    home_mine = jnp.logical_and(line_mine, plane_mine)

    def row_dest(i):
        return dev(x, y, (z + i) % 4, zl)

    def row_home(i):
        return dev(x, y, 2 * (i // 2) + core, i % 2), i

    def col_dest(i):
        m = (i // 4 + s) % 8
        return dev(m % 4, 2 * core + m // 4, (z + i) % 4, zh)

    def col_home(i):
        j = (s + i) % 32
        return (j, core * 2 + y // 2), j

    def plane_dest(i):
        x_, y_, core_ = (x + i) % 4, (y + (i // 4)) % 4, (core + i // 16) % 2
        return dev(x_, y_, z, core_), x_, y_, core_

    barrier = pltpu.get_barrier_semaphore()

    def greet(dest):
        @pl.when(jnp.logical_not(is_me(dest)))
        def _():
            pl.semaphore_signal(barrier, inc=1, device_id=dest, device_id_type=MESH)

    arrays = (q_row, k_row, q_col, k_col, out_grad, v_row)

    def load(n):
        return pltpu.make_async_copy(arrays[n], stage.at[n % 2], load_sem.at[n % 2])

    def pack_next(n):
        load(n).wait()
        pack(stage.at[n % 2], sends.at[n])
        if n + 2 < 6:
            load(n + 2).start()

    load(0).start()
    load(1).start()
    loop(6, lambda i: greet(dev(x, y, (z + 1 + i // 2) % 4, i % 2)))
    loop(31, lambda i: greet(plane_dest(i + 1)[0]))
    loop(32, lambda i: greet(col_dest(i)))
    loop(32, lambda i: greet(col_home(i)[0]))
    pack_next(0)
    pack_next(1)
    pack_next(2)
    pl.semaphore_wait(barrier, 101 - jnp.where(home_mine, 2, 0))

    def send_rows(n, dst):
        def body(i, maybe_me):
            z_ = (z + i) % 4
            push(sends.at[n, z_], dst.at[:, pl.ds(pl.multiple_of(g * 128, 128), 128), :],
                 in_send.at[n], in_recv.at[n], row_dest(i), maybe_me)

        fan(4, body)

    def send_plane(n, dst):
        def body(i, maybe_me):
            x_, half, core_ = (x + i) % 4, (y + i // 4) % 2, (core + i // 8) % 2
            push(sends.at[n, pl.ds(2 * core_, 2), :, pl.ds(pl.multiple_of((half * 4 + x_) * 16, 16), 16), :],
                 dst.at[:, chip], in_send.at[n], in_recv.at[n], dev(x_, 2 * core + half, z, core_), maybe_me)

        fan(16, body)

    def send_line(n, src, dst):
        def body(i, maybe_me):
            j = (i + zl) % 2
            push(src.at[j], dst.at[zl], on_send.at[n], on_recv.at[n], dev(x, y, 2 * core + j, zh), maybe_me)

        fan(2, body)

    def wait_in(n):
        if n in (0, 1, 5):
            wait_sent(in_send.at[n], lambda k: sends.at[n, 0:k], 4, row_mine)
        else:
            wait_sent(in_send.at[n], lambda k: mq.at[:, 0:k], 16, plane_mine)

    own_rows = pl.ds(pl.multiple_of(core * 256, 256), 256)
    other_rows = pl.ds(pl.multiple_of((1 - core) * 256, 256), 256)
    own_slab = pl.ds(pl.multiple_of(slab * 16, 16), 16)
    other_core = dev(x, y, z, 1 - core)

    def send_sum(src, dst, n):
        def body(i, maybe_me):
            dest, x_, y_, _ = plane_dest(i)
            push(src(y_ * 4 + x_), dst.at[chip], plane_send.at[n], plane_recv.at[n], dest, maybe_me)

        fan(16, body)

    def share(value, dst, n):
        dst[own_slab, :] = value.astype(BF16)
        loop(15, lambda i: push(dst.at[own_slab, :], dst.at[own_slab, :], plane_send.at[n], plane_recv.at[n],
                                plane_dest(i + 1)[0], False))

    def share_core(dst, n, core_n):
        for h in range(3):
            wait_for(dst.at[h, 0:240, :], plane_recv.at[n + h])
            push(dst.at[h, own_rows, :], dst.at[h, own_rows, :], core_send.at[core_n + h], core_recv.at[core_n + h],
                 other_core, False)
        for h in range(3):
            wait_for(dst.at[h, 0:256, :], core_recv.at[core_n + h])

    def products(a, b, inbox, core_n):
        for h in range(3):
            row_product(a, b, part, h)
            push(part.at[h, other_rows, :], inbox.at[h], core_send.at[core_n + h], core_recv.at[core_n + h], other_core, False)

    def add_up(ref):
        total = ref[0].astype(F32)
        for n in range(1, 16):
            total += ref[n].astype(F32)
        return total

    send_rows(0, rq)
    send_rows(1, rk)
    send_plane(2, mq)
    pack_next(3)
    send_plane(3, mk)
    pack_next(4)
    pack_next(5)
    wait_in(0)
    send_rows(5, rv)
    wait_in(2)
    send_plane(4, mo)

    wait_for(rq, in_recv.at[0])
    wait_for(rk, in_recv.at[1])
    products(rq, rk, core_l, 0)
    wait_for(mq, in_recv.at[2])
    send_line(0, mq, cq)
    for h in range(3):
        wait_for(core_l.at[h], core_recv.at[h])
        part[h, own_rows, :] += core_l[h]
        send_sum(lambda n: part.at[h, pl.ds(pl.multiple_of(core * 256 + n * 16, 16), 16), :], sum_l.at[h], h)
    wait_for(mk, in_recv.at[3])
    send_line(1, mk, ck)
    for h in range(3):
        wait_for(sum_l.at[h], plane_recv.at[h])
        logits = add_up(sum_l.at[h]) * ROW_SCALE
        weights = jnp.exp(logits - jnp.max(logits, axis=-1, keepdims=True))
        probs = weights / jnp.sum(weights, axis=-1, keepdims=True)
        tied_f[h] = probs
        share(probs, tied.at[h], 3 + h)
    wait_for(mo, in_recv.at[4])
    send_line(2, mo, co)
    share_core(tied, 3, 3)

    wait_for(rv, in_recv.at[5])
    wait_in(5)
    ro = sends.at[5]

    def put_ro(r2, tile, value):
        for b in range(4):
            ro[r2, b, :, tile * 128 : tile * 128 + 128] = value[128 * b : 128 * b + 128]

    mid, outer = pl.ds(256, 128), pl.ds(0, 256)

    def send_ro(lanes, n):
        def body(i, maybe_me):
            dest, x_, y_, core_ = plane_dest(i)
            t = core_ * 16 + y_ * 4 + x_
            push(ro.at[:, t // 8, pl.ds(pl.multiple_of((t % 8) * 16, 16), 16), lanes], cro.at[core, chip, :, :, lanes],
                 plane_send.at[n], plane_recv.at[n], dest, maybe_me)

        fan(32, body)

    apply_mid(tied, rv, put_ro, NN)
    send_ro(mid, 14)
    apply_outer(tied, rv, put_ro, NN)
    send_ro(outer, 6)

    for n in (1, 3, 4):
        wait_in(n)
    wait_for(cq, on_recv.at[0])
    by_column(cq, wide0, col_q)
    wait_for(ck, on_recv.at[1])
    by_column(ck, wide0, col_k)

    def put_probs(c, h, value):
        for half in range(2):
            rows = value[128 * half : 128 * half + 128]
            if h == 0:
                sends[c // 4, c % 4, half, :, 0:256] = rows
            elif h == 1:
                sends[c // 4, c % 4, half, :, 256:384] = rows[:, 0:128]
                sends[c // 4, c % 4, 2 + half, :, 0:128] = rows[:, 128:256]
            else:
                sends[c // 4, c % 4, 2 + half, :, 128:384] = rows

    def get_probs(c, h):
        rows = []
        for half in range(2):
            if h == 0:
                rows.append(sends[c // 4, c % 4, half, :, 0:256])
            elif h == 1:
                rows.append(jnp.concatenate([sends[c // 4, c % 4, half, :, 256:384], sends[c // 4, c % 4, 2 + half, :, 0:128]], axis=1))
            else:
                rows.append(sends[c // 4, c % 4, 2 + half, :, 128:384])
        return jnp.concatenate(rows, axis=0)

    def probs_pass(c):
        logs = []
        for h, (rows, low) in enumerate(HEADS):
            scores = dot(rows(col_k, c), keep(rows(col_q, c), low), NT) * COL_SCALE
            top = jnp.max(scores, axis=0, keepdims=True)
            weights = jnp.exp(scores - top)
            total = jnp.sum(weights, axis=0, keepdims=True)
            put_probs(c, h, (weights * (1.0 / total)).astype(BF16))
            logs.append(top + jnp.log(total))
        norms[c] = jnp.concatenate(logs, axis=0)

    columns(probs_pass)

    wait_for(co, on_recv.at[2])
    by_column(co, wide0, col_o)

    def mixed_pass(c):
        outer = outer_rows(col_o, c)
        put_outer(wide1, c, dot(get_probs(c, 0), outer, NN), dot(get_probs(c, 1), outer, NN))
        put_mid(wide1, c, dot(get_probs(c, 2), mid_rows(col_o, c), NN))

    columns(mixed_pass)
    by_row(wide1, cq, (0, 1, 2))

    def send_mixed(i, maybe_me):
        dest, x_, y_, core_ = plane_dest(i)
        push(cq.at[core_, y_ * 4 + x_], rmix.at[:, own_slab, :], plane_send.at[7], plane_recv.at[7], dest, maybe_me)

    fan(32, send_mixed)

    wait_for(cro.at[:, :, :, :, mid], plane_recv.at[14])
    by_column(cro, wide0, col_r, (2,))

    def slope_parts(c, h):
        rows, low = HEADS[h]
        queries, keys = rows(col_q, c), rows(col_k, c)
        scores = dot(keys, keep(queries, low), NT) * COL_SCALE
        probs = jnp.exp(scores - norms[c, h : h + 1, :])
        grads = dot(rows(col_r, c), keep(rows(col_o, c), low), NT)
        slope = probs * (grads - jnp.sum(probs * grads, axis=0, keepdims=True))
        slope = slope.astype(BF16)
        return dot(slope, keys, TN) * COL_SCALE, dot(slope, queries, NN) * COL_SCALE

    def mid_pass(c):
        q_part, k_part = slope_parts(c, 2)
        put_mid(wide0, c, q_part)
        put_mid(wide1, c, k_part)

    def outer_pass(c):
        q_p, k_p = slope_parts(c, 0)
        q_q, k_q = slope_parts(c, 1)
        put_outer(wide0, c, q_p, q_q)
        put_outer(wide1, c, k_p, k_q)

    def send_home(src, dst, n, lanes):
        def body(i, maybe_me):
            dest, j = col_home(i)
            push(src.at[j % 2, j // 2, :, :, lanes],
                 dst.at[z, :, pl.ds(pl.multiple_of((slab % 8) * 16, 16), 16), lanes],
                 out_send.at[n], out_recv.at[n], dest, maybe_me)

        fan(32, body)

    columns(mid_pass)
    by_row(wide0, ck, (2,))
    send_home(ck, o_qc, 5, mid)
    by_row(wide1, co, (2,))
    send_home(co, o_kc, 6, mid)
    wait_for(cro.at[:, :, :, :, outer], plane_recv.at[6])
    by_column(cro, wide0, col_r, (0, 1))
    columns(outer_pass)
    by_row(wide0, ck, (0, 1))
    send_home(ck, o_qc, 3, outer)
    by_row(wide1, co, (0, 1))

    wait_for(rmix, plane_recv.at[7])
    for h in range(3):
        wait_for(part.at[h, 0:256, :], core_send.at[h])
        wait_for(sum_l.at[h, 0:15], plane_send.at[h])
    products(rmix, rv, core_g, 6)

    def in_place(ref):
        def store(r2, tile, value):
            ref[r2, :, tile * 128 : tile * 128 + 128] = value

        return store

    def send_rows_home(src, dst, n):
        def body(i):
            dest, b = row_home(i)
            push(src.at[:, pl.ds(pl.multiple_of(b * 128, 128), 128), :], dst.at[z], out_send.at[n], out_recv.at[n], dest)

        loop(4, body)

    for h in range(3):
        wait_for(core_g.at[h], core_recv.at[6 + h])
        half_g[h] = (part[h, own_rows, :] + core_g[h]).astype(BF16)
        send_sum(lambda n: half_g.at[h, pl.ds(pl.multiple_of(n * 16, 16), 16), :], sum_g.at[h], 8 + h)
    row_apply(tied, rmix, in_place(rmix), TN)
    send_rows_home(rmix, o_vr, 2)
    for h in range(3):
        wait_for(sum_g.at[h], plane_recv.at[8 + h])
        grads = add_up(sum_g.at[h])
        probs = tied_f[h]
        share(probs * (grads - jnp.sum(probs * grads, axis=-1, keepdims=True)), slopes.at[h], 11 + h)
    send_home(co, o_kc, 4, outer)
    share_core(slopes, 11, 9)

    row_apply(slopes, rk, in_place(rk), NN, ROW_SCALE)
    send_rows_home(rk, o_qr, 0)
    row_apply(slopes, rq, in_place(rq), TN, ROW_SCALE)
    send_rows_home(rq, o_kr, 1)

    for n in range(3):
        wait_sent(on_send.at[n], lambda k: mq.at[0:k], 2, line_mine)
    wait_for(rq.at[:, 0:496, outer], plane_send.at[6])
    wait_for(rq.at[:, 0:496, mid], plane_send.at[14])
    wait_for(rq.at[:, 0:496, :], plane_send.at[7])
    for h in range(3):
        wait_for(tied.at[h, 0:240, :], plane_send.at[3 + h])
        wait_for(sum_g.at[h, 0:15], plane_send.at[8 + h])
        wait_for(tied.at[h, 0:240, :], plane_send.at[11 + h])
        wait_for(tied.at[h, 0:256, :], core_send.at[3 + h])
        wait_for(core_g.at[h], core_send.at[6 + h])
        wait_for(tied.at[h, 0:256, :], core_send.at[9 + h])
    for n, ref in enumerate((o_qr, o_kr, o_vr)):
        wait_sent(out_send.at[n], lambda k: sends.at[0, 0:k], 4, row_mine)
        wait_for(ref, out_recv.at[n])
    for n, ref, lanes in ((5, o_qc, mid), (6, o_kc, mid), (3, o_qc, outer), (4, o_kc, outer)):
        wait_sent(out_send.at[n], lambda k: rq.at[:, 0 : 16 * k, lanes], 32, home_mine)
        wait_for(ref.at[:, :, :, lanes], out_recv.at[n])


def on_device(q_row, k_row, v_row, q_col, k_col, out_grad):
    vm = pltpu.VMEM
    dma = pltpu.SemaphoreType.DMA
    rows, cols = (4, 512, 384), (2, 16, 4, 16, 384)
    packed = pl.pallas_call(
        main_kernel,
        name="layer",
        out_shape=[jax.ShapeDtypeStruct((4, 4, 128, 384), BF16)] * 5,
        in_specs=[pl.BlockSpec(memory_space=pl.ANY)] * 6,
        out_specs=[pl.BlockSpec(memory_space=pl.ANY)] * 5,
        scratch_shapes=[
            vm((2, 8, 128, 768), BF16),
            vm((6, 4, 4, 128, 384), BF16),
            vm(rows, BF16), vm(rows, BF16), vm(rows, BF16),
            vm(cols, BF16), vm(cols, BF16), vm(cols, BF16),
            vm(cols, BF16), vm(cols, BF16), vm(cols, BF16), vm(cols, BF16),
            vm(rows, BF16),
            vm((3, 512, 512), F32),
            vm((3, 256, 512), F32), vm((3, 256, 512), F32),
            vm((3, 16, 16, 512), F32),
            vm((3, 256, 512), BF16),
            vm((3, 16, 16, 512), BF16),
            vm((3, 16, 512), F32),
            vm((3, 512, 512), BF16), vm((3, 512, 512), BF16),
            vm((3, 2048, 128), F32), vm((3, 2048, 128), F32),
            vm((16, 256, 256), BF16), vm((16, 256, 256), BF16), vm((16, 256, 256), BF16), vm((16, 256, 256), BF16),
            vm((16, 3, 256), F32),
            dma((2,)), dma((6,)), dma((6,)), dma((3,)), dma((3,)), dma((15,)), dma((15,)), dma((12,)), dma((12,)),
            dma((7,)), dma((7,)),
        ],
        compiler_params=pltpu.CompilerParams(collective_id=0, has_side_effects=True, vmem_limit_bytes=62 << 20),
    )(q_row, k_row, v_row, q_col, k_col, out_grad)
    return unpack(packed)


def solution(mesh):
    spec = P("seq", "col", None)
    return jax.shard_map(on_device, mesh=mesh, in_specs=(spec,) * 6, out_specs=(spec,) * 5, check_vma=False)
```

```python
import math

import jax
import jax.numpy as jnp
from jax import lax
from jax.experimental import pallas as pl
from jax.experimental.pallas import tpu as pltpu
from jax.sharding import PartitionSpec as P

MESH = pl.DeviceIdType.MESH
F32 = jnp.float32
BF16 = jnp.bfloat16
NT = (((1,), (1,)), ((), ()))
NN = (((1,), (0,)), ((), ()))
TN = (((0,), (0,)), ((), ()))
ROW_SCALE = 1.0 / math.sqrt(16384.0)
COL_SCALE = 1.0 / math.sqrt(64.0)


def dot(a, b, dims):
    return lax.dot_general(a, b, dims, preferred_element_type=F32)


def swap_halves(t):
    return jnp.concatenate([t[..., 64:128], t[..., 0:64]], axis=-1)


def low_lanes(shape):
    return lax.broadcasted_iota(jnp.int32, shape, len(shape) - 1) % 128 < 64


def pack(src, dst):
    lo = low_lanes((128, 128))

    def step(r2, _):
        for half in range(2):
            base = half * 384
            mid_a, mid_b = src[r2, :, base + 128 : base + 256], src[r2 + 4, :, base + 128 : base + 256]
            turned = swap_halves(mid_b)
            even, odd = 2 * half, 2 * half + 1
            dst[even, r2, :, 0:128] = src[r2, :, base : base + 128]
            dst[even, r2, :, 128:256] = src[r2 + 4, :, base : base + 128]
            dst[even, r2, :, 256:384] = jnp.where(lo, mid_a, turned)
            dst[odd, r2, :, 0:128] = src[r2, :, base + 256 : base + 384]
            dst[odd, r2, :, 128:256] = src[r2 + 4, :, base + 256 : base + 384]
            dst[odd, r2, :, 256:384] = jnp.where(lo, turned, mid_a)
        return 0

    lax.fori_loop(0, 4, step, 0)


def unpack_kernel(*refs):
    lo = low_lanes((128, 128))
    for src, dst in zip(refs[:5], refs[5:]):
        for half, k in ((0, 0), (0, 1), (1, 0), (1, 1)):
            base = half * 384
            even, odd = 2 * half, 2 * half + 1
            mid_even, mid_odd = src[even, k, :, 256:384], src[odd, k, :, 256:384]
            dst[0, k, :, base : base + 128] = src[even, k, :, 0:128]
            dst[1, k, :, base : base + 128] = src[even, k, :, 128:256]
            dst[0, k, :, base + 128 : base + 256] = jnp.where(lo, mid_even, mid_odd)
            dst[1, k, :, base + 128 : base + 256] = swap_halves(jnp.where(lo, mid_odd, mid_even))
            dst[0, k, :, base + 256 : base + 384] = src[odd, k, :, 0:128]
            dst[1, k, :, base + 256 : base + 384] = src[odd, k, :, 128:256]


def unpack(packed):
    outs = pl.pallas_call(
        unpack_kernel,
        name="unpack",
        grid=(2,),
        out_shape=[jax.ShapeDtypeStruct((2, 4, 128, 768), BF16)] * 5,
        in_specs=[pl.BlockSpec((4, 2, 128, 384), lambda i: (0, i, 0, 0))] * 5,
        out_specs=[pl.BlockSpec((2, 2, 128, 768), lambda i: (0, i, 0, 0))] * 5,
        compiler_params=pltpu.CompilerParams(vmem_limit_bytes=62 << 20),
    )(*packed)
    return tuple(o.reshape(8, 128, 768) for o in outs)


def row_product(a, b, out, h):
    low = low_lanes((512, 512))
    zero = jnp.zeros((512, 512), BF16)
    total = None
    if h < 2:
        for u in (0, 2):
            left = jnp.concatenate([a[u, :, 0:256], a[u + 1, :, 0:256]], axis=1)
            right = jnp.concatenate([b[u, :, 0:256], b[u + 1, :, 0:256]], axis=1)
            left = jnp.where(low, left, zero) if h == 0 else jnp.where(low, zero, left)
            term = dot(left, right, NT)
            total = term if total is None else total + term
    else:
        left = jnp.concatenate([a[u, :, 256:384] for u in range(4)], axis=1)
        right = jnp.concatenate([b[u, :, 256:384] for u in range(4)], axis=1)
        total = dot(left, right, NT)
    out[h] = total


def finish(value, scale):
    return (value if scale is None else value * scale).astype(BF16)


def apply_outer(m, b, store, dims, scale=None):
    low = low_lanes((512, 256))

    def step(pair, _):
        for r2 in (2 * pair, 2 * pair + 1):
            right = b[r2, :, 0:256]
            both = finish(jnp.where(low, dot(m[0], right, dims), dot(m[1], right, dims)), scale)
            store(r2, 0, both[:, 0:128])
            store(r2, 1, both[:, 128:256])
        return 0

    lax.fori_loop(0, 2, step, 0)


def apply_mid(m, b, store, dims, scale=None):
    def step(pair, _):
        right = jnp.concatenate([b[2 * pair, :, 256:384], b[2 * pair + 1, :, 256:384]], axis=1)
        third = finish(dot(m[2], right, dims), scale)
        store(2 * pair, 2, third[:, 0:128])
        store(2 * pair + 1, 2, third[:, 128:256])
        return 0

    lax.fori_loop(0, 2, step, 0)


def row_apply(*args):
    apply_outer(*args)
    apply_mid(*args)


def by_column(src, wide, dst, tiles=(0, 1, 2)):
    def widen(i, _):
        for t in tiles:
            block = src[i // 4, pl.ds((i % 4) * 4, 4), :, :, 128 * t : 128 * t + 128]
            wide[t, pl.ds(pl.multiple_of(i * 256, 256), 256), :] = block.reshape(256, 128).astype(F32)
        return 0

    lax.fori_loop(0, 8, widen, 0)

    def gather(i, _):
        for c in (2 * i, 2 * i + 1):
            rows = pl.ds(c, 128, stride=16)
            for t in tiles:
                if t < 2:
                    dst[c, 128 * t : 128 * t + 128, 0:128] = wide[t, rows, :].astype(BF16)
                else:
                    mid = wide[2, rows, :]
                    dst[c, 0:128, 128:256] = mid.astype(BF16)
                    dst[c, 128:256, 128:256] = pltpu.roll(mid, 64, 1).astype(BF16)
        return 0

    lax.fori_loop(0, 8, gather, 0)


def by_row(wide, dst, tiles):
    def narrow(i, _):
        for t in tiles:
            block = wide[t, pl.ds(pl.multiple_of(i * 256, 256), 256), :].astype(BF16)
            dst[i // 4, pl.ds((i % 4) * 4, 4), :, :, 128 * t : 128 * t + 128] = block.reshape(4, 4, 16, 128)
        return 0

    lax.fori_loop(0, 8, narrow, 0)


def outer_rows(ref, c):
    return ref[c, :, 0:128]


def mid_rows(ref, c):
    return ref[c, :, 128:256]


def keep(x, low):
    lo = low_lanes(x.shape)
    zero = jnp.zeros_like(x)
    return jnp.where(lo, x, zero) if low else jnp.where(lo, zero, x)


HEADS = ((outer_rows, True), (outer_rows, False), (mid_rows, True))


def put_outer(wide, c, p_part, q_part):
    outer = jnp.where(low_lanes((256, 128)), p_part, q_part)
    rows = pl.ds(c, 128, stride=16)
    wide[0, rows, :] = outer[0:128]
    wide[1, rows, :] = outer[128:256]


def put_mid(wide, c, part):
    wide[2, pl.ds(c, 128, stride=16), :] = jnp.where(low_lanes((128, 128)), part[0:128], pltpu.roll(part[128:256], 64, 1))


def main_kernel(
    q_row, k_row, v_row, q_col, k_col, out_grad,
    o_qr, o_kr, o_vr, o_qc, o_kc,
    stage, sends, rq, rk, rv, mq, mk, mo, cq, ck, co, cro, rmix,
    part, core_l, core_g, sum_l, half_g, sum_g, tied_f, tied, slopes,
    wide0, wide1, col_q, col_k, col_o, col_r, norms,
    load_sem, in_send, in_recv, on_send, on_recv, plane_send, plane_recv, core_send, core_recv, out_send, out_recv,
):
    s, g = lax.axis_index("seq"), lax.axis_index("col")
    x, y, zl = (s // 2) % 4, s // 8, s % 2
    zh, core = g // 2, g % 2
    z = 2 * zh + zl
    chip = y * 4 + x
    slab = core * 16 + chip

    def dev(x_, y_, z_, core_):
        return (y_ * 8 + x_ * 2 + z_ % 2, (z_ // 2) * 2 + core_)

    def is_me(d):
        return jnp.logical_and(d[0] == s, d[1] == g)

    def push(src, dst, send_sem, recv_sem, dest, maybe_me=True):
        def remote():
            pltpu.make_async_remote_copy(
                src_ref=src, dst_ref=dst, send_sem=send_sem, recv_sem=recv_sem, device_id=dest, device_id_type=MESH
            ).start()

        if not maybe_me:
            remote()
            return
        me = is_me(dest)
        pl.when(jnp.logical_not(me))(remote)

        @pl.when(me)
        def _():
            pltpu.make_async_copy(src, dst, recv_sem).start()

    def wait_for(ref, sem):
        pltpu.make_async_copy(ref, ref, sem).wait()

    def wait_sent(sem, chunks, count, mine):
        @pl.when(mine)
        def _():
            wait_for(chunks(count - 1), sem)

        @pl.when(jnp.logical_not(mine))
        def _():
            wait_for(chunks(count), sem)

    def loop(n, body):
        def step(i, _):
            body(i)
            return 0

        lax.fori_loop(0, n, step, 0)

    def columns(body):
        def four(i):
            for j in range(4):
                body(4 * i + j)

        loop(4, four)

    def fan(n, body):
        body(0, True)
        loop(n - 1, lambda i: body(i + 1, False))

    row_mine = core == zl
    plane_mine = y // 2 == core
    line_mine = core == zh
    home_mine = jnp.logical_and(line_mine, plane_mine)

    def row_dest(i):
        return dev(x, y, (z + i) % 4, zl)

    def row_home(i):
        return dev(x, y, 2 * (i // 2) + core, i % 2), i

    def col_dest(i):
        m = (i // 4 + s) % 8
        return dev(m % 4, 2 * core + m // 4, (z + i) % 4, zh)

    def col_home(i):
        j = (s + i) % 32
        return (j, core * 2 + y // 2), j

    def plane_dest(i):
        x_, y_, core_ = (x + i) % 4, (y + (i // 4)) % 4, (core + i // 16) % 2
        return dev(x_, y_, z, core_), x_, y_, core_

    barrier = pltpu.get_barrier_semaphore()

    def greet(dest):
        @pl.when(jnp.logical_not(is_me(dest)))
        def _():
            pl.semaphore_signal(barrier, inc=1, device_id=dest, device_id_type=MESH)

    arrays = (q_row, k_row, q_col, k_col, out_grad, v_row)

    def load(n):
        return pltpu.make_async_copy(arrays[n], stage.at[n % 2], load_sem.at[n % 2])

    def pack_next(n):
        load(n).wait()
        pack(stage.at[n % 2], sends.at[n])
        if n + 2 < 6:
            load(n + 2).start()

    load(0).start()
    load(1).start()
    loop(6, lambda i: greet(dev(x, y, (z + 1 + i // 2) % 4, i % 2)))
    loop(31, lambda i: greet(plane_dest(i + 1)[0]))
    pack_next(0)
    pack_next(1)
    pack_next(2)
    pl.semaphore_wait(barrier, 37)

    def send_rows(n, dst):
        def body(i, maybe_me):
            z_ = (z + i) % 4
            push(sends.at[n, z_], dst.at[:, pl.ds(pl.multiple_of(g * 128, 128), 128), :],
                 in_send.at[n], in_recv.at[n], row_dest(i), maybe_me)

        fan(4, body)

    def send_plane(n, dst):
        def body(i, maybe_me):
            x_, half, core_ = (x + i) % 4, (y + i // 4) % 2, (core + i // 8) % 2
            push(sends.at[n, pl.ds(2 * core_, 2), :, pl.ds(pl.multiple_of((half * 4 + x_) * 16, 16), 16), :],
                 dst.at[:, chip], in_send.at[n], in_recv.at[n], dev(x_, 2 * core + half, z, core_), maybe_me)

        fan(16, body)

    def send_line(n, src, dst):
        def body(i, maybe_me):
            j = (i + zl) % 2
            push(src.at[j], dst.at[zl], on_send.at[n], on_recv.at[n], dev(x, y, 2 * core + j, zh), maybe_me)

        fan(2, body)

    def wait_in(n):
        if n in (0, 1, 5):
            wait_sent(in_send.at[n], lambda k: sends.at[n, 0:k], 4, row_mine)
        else:
            wait_sent(in_send.at[n], lambda k: mq.at[:, 0:k], 16, plane_mine)

    own_rows = pl.ds(pl.multiple_of(core * 256, 256), 256)
    other_rows = pl.ds(pl.multiple_of((1 - core) * 256, 256), 256)
    own_slab = pl.ds(pl.multiple_of(slab * 16, 16), 16)
    other_core = dev(x, y, z, 1 - core)

    def send_sum(src, dst, n):
        def body(i, maybe_me):
            dest, x_, y_, _ = plane_dest(i)
            push(src(y_ * 4 + x_), dst.at[chip], plane_send.at[n], plane_recv.at[n], dest, maybe_me)

        fan(16, body)

    def share(value, dst, n):
        dst[own_slab, :] = value.astype(BF16)
        loop(15, lambda i: push(dst.at[own_slab, :], dst.at[own_slab, :], plane_send.at[n], plane_recv.at[n],
                                plane_dest(i + 1)[0], False))

    def share_core(dst, n, core_n):
        for h in range(3):
            wait_for(dst.at[h, 0:240, :], plane_recv.at[n + h])
            push(dst.at[h, own_rows, :], dst.at[h, own_rows, :], core_send.at[core_n + h], core_recv.at[core_n + h],
                 other_core, False)
        for h in range(3):
            wait_for(dst.at[h, 0:256, :], core_recv.at[core_n + h])

    def products(a, b, inbox, core_n):
        for h in range(3):
            row_product(a, b, part, h)
            push(part.at[h, other_rows, :], inbox.at[h], core_send.at[core_n + h], core_recv.at[core_n + h], other_core, False)

    def add_up(ref):
        total = ref[0].astype(F32)
        for n in range(1, 16):
            total += ref[n].astype(F32)
        return total

    send_rows(0, rq)
    send_rows(1, rk)
    send_plane(2, mq)
    pack_next(3)
    send_plane(3, mk)
    pack_next(4)
    pack_next(5)
    wait_in(0)
    send_rows(5, rv)
    wait_in(2)
    send_plane(4, mo)

    wait_for(rq, in_recv.at[0])
    wait_for(rk, in_recv.at[1])
    products(rq, rk, core_l, 0)
    wait_for(mq, in_recv.at[2])
    send_line(0, mq, cq)
    for h in range(3):
        wait_for(core_l.at[h], core_recv.at[h])
        part[h, own_rows, :] += core_l[h]
        send_sum(lambda n: part.at[h, pl.ds(pl.multiple_of(core * 256 + n * 16, 16), 16), :], sum_l.at[h], h)
    wait_for(mk, in_recv.at[3])
    send_line(1, mk, ck)
    for h in range(3):
        wait_for(sum_l.at[h], plane_recv.at[h])
        logits = add_up(sum_l.at[h]) * ROW_SCALE
        weights = jnp.exp(logits - jnp.max(logits, axis=-1, keepdims=True))
        probs = weights / jnp.sum(weights, axis=-1, keepdims=True)
        tied_f[h] = probs
        share(probs, tied.at[h], 3 + h)
    wait_for(mo, in_recv.at[4])
    send_line(2, mo, co)
    share_core(tied, 3, 3)

    wait_for(rv, in_recv.at[5])
    wait_in(5)
    ro = sends.at[5]

    def put_ro(r2, tile, value):
        for b in range(4):
            ro[r2, b, :, tile * 128 : tile * 128 + 128] = value[128 * b : 128 * b + 128]

    mid, outer = pl.ds(256, 128), pl.ds(0, 256)

    def send_ro(lanes, n):
        def body(i, maybe_me):
            dest, x_, y_, core_ = plane_dest(i)
            t = core_ * 16 + y_ * 4 + x_
            push(ro.at[:, t // 8, pl.ds(pl.multiple_of((t % 8) * 16, 16), 16), lanes], cro.at[core, chip, :, :, lanes],
                 plane_send.at[n], plane_recv.at[n], dest, maybe_me)

        fan(32, body)

    apply_mid(tied, rv, put_ro, NN)
    send_ro(mid, 14)
    apply_outer(tied, rv, put_ro, NN)
    send_ro(outer, 6)

    for n in (1, 3, 4):
        wait_in(n)
    wait_for(cq, on_recv.at[0])
    by_column(cq, wide0, col_q)
    wait_for(ck, on_recv.at[1])
    by_column(ck, wide0, col_k)

    def put_probs(c, h, value):
        for half in range(2):
            rows = value[128 * half : 128 * half + 128]
            if h == 0:
                sends[c // 4, c % 4, half, :, 0:256] = rows
            elif h == 1:
                sends[c // 4, c % 4, half, :, 256:384] = rows[:, 0:128]
                sends[c // 4, c % 4, 2 + half, :, 0:128] = rows[:, 128:256]
            else:
                sends[c // 4, c % 4, 2 + half, :, 128:384] = rows

    def get_probs(c, h):
        rows = []
        for half in range(2):
            if h == 0:
                rows.append(sends[c // 4, c % 4, half, :, 0:256])
            elif h == 1:
                rows.append(jnp.concatenate([sends[c // 4, c % 4, half, :, 256:384], sends[c // 4, c % 4, 2 + half, :, 0:128]], axis=1))
            else:
                rows.append(sends[c // 4, c % 4, 2 + half, :, 128:384])
        return jnp.concatenate(rows, axis=0)

    def probs_pass(c):
        logs = []
        for h, (rows, low) in enumerate(HEADS):
            scores = dot(rows(col_k, c), keep(rows(col_q, c), low), NT) * COL_SCALE
            top = jnp.max(scores, axis=0, keepdims=True)
            weights = jnp.exp(scores - top)
            total = jnp.sum(weights, axis=0, keepdims=True)
            put_probs(c, h, (weights * (1.0 / total)).astype(BF16))
            logs.append(top + jnp.log(total))
        norms[c] = jnp.concatenate(logs, axis=0)

    columns(probs_pass)

    wait_for(co, on_recv.at[2])
    by_column(co, wide0, col_o)

    def mixed_pass(c):
        outer = outer_rows(col_o, c)
        put_outer(wide1, c, dot(get_probs(c, 0), outer, NN), dot(get_probs(c, 1), outer, NN))
        put_mid(wide1, c, dot(get_probs(c, 2), mid_rows(col_o, c), NN))

    columns(mixed_pass)
    by_row(wide1, cq, (0, 1, 2))

    def send_mixed(i, maybe_me):
        dest, x_, y_, core_ = plane_dest(i)
        push(cq.at[core_, y_ * 4 + x_], rmix.at[:, own_slab, :], plane_send.at[7], plane_recv.at[7], dest, maybe_me)

    fan(32, send_mixed)

    wait_for(cro.at[:, :, :, :, mid], plane_recv.at[14])
    by_column(cro, wide0, col_r, (2,))

    def slope_parts(c, h):
        rows, low = HEADS[h]
        queries, keys = rows(col_q, c), rows(col_k, c)
        scores = dot(keys, keep(queries, low), NT) * COL_SCALE
        probs = jnp.exp(scores - norms[c, h : h + 1, :])
        grads = dot(rows(col_r, c), keep(rows(col_o, c), low), NT)
        slope = probs * (grads - jnp.sum(probs * grads, axis=0, keepdims=True))
        slope = slope.astype(BF16)
        return dot(slope, keys, TN) * COL_SCALE, dot(slope, queries, NN) * COL_SCALE

    def mid_pass(c):
        q_part, k_part = slope_parts(c, 2)
        put_mid(wide0, c, q_part)
        put_mid(wide1, c, k_part)

    def outer_pass(c):
        q_p, k_p = slope_parts(c, 0)
        q_q, k_q = slope_parts(c, 1)
        put_outer(wide0, c, q_p, q_q)
        put_outer(wide1, c, k_p, k_q)

    def send_home(src, dst, n, lanes):
        def body(i, maybe_me):
            dest, j = col_home(i)
            push(src.at[j % 2, j // 2, :, :, lanes],
                 dst.at[z, :, pl.ds(pl.multiple_of((slab % 8) * 16, 16), 16), lanes],
                 out_send.at[n], out_recv.at[n], dest, maybe_me)

        fan(32, body)

    columns(mid_pass)
    by_row(wide0, ck, (2,))
    send_home(ck, o_qc, 5, mid)
    by_row(wide1, co, (2,))
    send_home(co, o_kc, 6, mid)
    wait_for(cro.at[:, :, :, :, outer], plane_recv.at[6])
    by_column(cro, wide0, col_r, (0, 1))
    columns(outer_pass)
    by_row(wide0, ck, (0, 1))
    send_home(ck, o_qc, 3, outer)
    by_row(wide1, co, (0, 1))

    wait_for(rmix, plane_recv.at[7])
    for h in range(3):
        wait_for(part.at[h, 0:256, :], core_send.at[h])
        wait_for(sum_l.at[h, 0:15], plane_send.at[h])
    products(rmix, rv, core_g, 6)

    def in_place(ref):
        def store(r2, tile, value):
            ref[r2, :, tile * 128 : tile * 128 + 128] = value

        return store

    def send_rows_home(src, dst, n):
        def body(i):
            dest, b = row_home(i)
            push(src.at[:, pl.ds(pl.multiple_of(b * 128, 128), 128), :], dst.at[z], out_send.at[n], out_recv.at[n], dest)

        loop(4, body)

    for h in range(3):
        wait_for(core_g.at[h], core_recv.at[6 + h])
        half_g[h] = (part[h, own_rows, :] + core_g[h]).astype(BF16)
        send_sum(lambda n: half_g.at[h, pl.ds(pl.multiple_of(n * 16, 16), 16), :], sum_g.at[h], 8 + h)
    row_apply(tied, rmix, in_place(rmix), TN)
    send_rows_home(rmix, o_vr, 2)
    for h in range(3):
        wait_for(sum_g.at[h], plane_recv.at[8 + h])
        grads = add_up(sum_g.at[h])
        probs = tied_f[h]
        share(probs * (grads - jnp.sum(probs * grads, axis=-1, keepdims=True)), slopes.at[h], 11 + h)
    send_home(co, o_kc, 4, outer)
    share_core(slopes, 11, 9)

    row_apply(slopes, rk, in_place(rk), NN, ROW_SCALE)
    send_rows_home(rk, o_qr, 0)
    row_apply(slopes, rq, in_place(rq), TN, ROW_SCALE)
    send_rows_home(rq, o_kr, 1)

    for n in range(3):
        wait_sent(on_send.at[n], lambda k: mq.at[0:k], 2, line_mine)
    wait_for(rq.at[:, 0:496, outer], plane_send.at[6])
    wait_for(rq.at[:, 0:496, mid], plane_send.at[14])
    wait_for(rq.at[:, 0:496, :], plane_send.at[7])
    for h in range(3):
        wait_for(tied.at[h, 0:240, :], plane_send.at[3 + h])
        wait_for(sum_g.at[h, 0:15], plane_send.at[8 + h])
        wait_for(tied.at[h, 0:240, :], plane_send.at[11 + h])
        wait_for(tied.at[h, 0:256, :], core_send.at[3 + h])
        wait_for(core_g.at[h], core_send.at[6 + h])
        wait_for(tied.at[h, 0:256, :], core_send.at[9 + h])
    for n, ref in enumerate((o_qr, o_kr, o_vr)):
        wait_sent(out_send.at[n], lambda k: sends.at[0, 0:k], 4, row_mine)
        wait_for(ref, out_recv.at[n])
    for n, ref, lanes in ((5, o_qc, mid), (6, o_kc, mid), (3, o_qc, outer), (4, o_kc, outer)):
        wait_sent(out_send.at[n], lambda k: rq.at[:, 0 : 16 * k, lanes], 32, home_mine)
        wait_for(ref.at[:, :, :, lanes], out_recv.at[n])


def on_device(q_row, k_row, v_row, q_col, k_col, out_grad):
    vm = pltpu.VMEM
    dma = pltpu.SemaphoreType.DMA
    rows, cols = (4, 512, 384), (2, 16, 4, 16, 384)
    packed = pl.pallas_call(
        main_kernel,
        name="layer",
        out_shape=[jax.ShapeDtypeStruct((4, 4, 128, 384), BF16)] * 5,
        in_specs=[pl.BlockSpec(memory_space=pl.ANY)] * 6,
        out_specs=[pl.BlockSpec(memory_space=pl.ANY)] * 5,
        scratch_shapes=[
            vm((2, 8, 128, 768), BF16),
            vm((6, 4, 4, 128, 384), BF16),
            vm(rows, BF16), vm(rows, BF16), vm(rows, BF16),
            vm(cols, BF16), vm(cols, BF16), vm(cols, BF16),
            vm(cols, BF16), vm(cols, BF16), vm(cols, BF16), vm(cols, BF16),
            vm(rows, BF16),
            vm((3, 512, 512), F32),
            vm((3, 256, 512), F32), vm((3, 256, 512), F32),
            vm((3, 16, 16, 512), F32),
            vm((3, 256, 512), BF16),
            vm((3, 16, 16, 512), BF16),
            vm((3, 16, 512), F32),
            vm((3, 512, 512), BF16), vm((3, 512, 512), BF16),
            vm((3, 2048, 128), F32), vm((3, 2048, 128), F32),
            vm((16, 256, 256), BF16), vm((16, 256, 256), BF16), vm((16, 256, 256), BF16), vm((16, 256, 256), BF16),
            vm((16, 3, 256), F32),
            dma((2,)), dma((6,)), dma((6,)), dma((3,)), dma((3,)), dma((15,)), dma((15,)), dma((12,)), dma((12,)),
            dma((7,)), dma((7,)),
        ],
        compiler_params=pltpu.CompilerParams(collective_id=0, has_side_effects=True, vmem_limit_bytes=62 << 20),
    )(q_row, k_row, v_row, q_col, k_col, out_grad)
    return unpack(packed)


def solution(mesh):
    spec = P("seq", "col", None)
    return jax.shard_map(on_device, mesh=mesh, in_specs=(spec,) * 6, out_specs=(spec,) * 5, check_vma=False)
```
